256 devices in a mesh: replica: 16 (over z, x_hi), shard: 16 (over y, x_lo, core).
Axes of the slice: x: 4 (x_hi: 2, x_lo: 2; x = x_hi * 2 + x_lo), y: 4, z: 8, core: 2. Of those that a mesh axis runs over, the one named last changes fastest.
Arguments:
- params: float32 [16, 4096, 1024], P('replica', 'shard'), may hold values from -0.09375 to 0.09375
- first_moment: float32 [16, 4096, 1024], P('replica', 'shard'), may hold values from -6 to 6
- second_moment: float32 [16, 4096, 1024], P('replica', 'shard'), may hold values from 0.02 to 0.5
- push_weight: float32 [16], P('replica'), may hold values from 0.5 to 2
- tokens: bfloat16 [16, 8192, 4096], P('replica', 'shard'), may hold values from -6 to 6
- cotangent: bfloat16 [16, 8192, 1024], P('replica', 'shard'), may hold values from -0.1796875 to 0.1796875
- gossip_round: int32 [1], replicated, may hold values from 0 to 15
Outputs:
- new_params: float32 [16, 4096, 1024], P('replica', 'shard')
- new_first: float32 [16, 4096, 1024], P('replica', 'shard')
- new_second: float32 [16, 4096, 1024], P('replica', 'shard')
- new_weight: float32 [16], P('replica')
- activation: bfloat16 [16, 8192, 1024], P('replica', 'shard')
The draws below stay inside these ranges and needn't reach their ends.
All inputs are finite; a program needn't handle non-finite values.
Results may differ from the reference program's by a relative error of at most 0.009.
Values may be sent and summed in bfloat16 or wider, within the bound.
A program may use at most 128 MiB of HBM per device.

```python
import math
import jax
import jax.numpy as jnp
from jax import lax

D = 4096
FF = 1024
STEP_COUNT = 20
REPLICAS = 16
TOKENS = 8192


def with_spikes(result, stream_key, source, target, blocks, factor):
    owner, partner = [(jnp.arange(result.shape[dim]) // (result.shape[dim] // blocks)).reshape([-1 if axis == dim else 1 for axis in range(result.ndim)]) for dim in (source, target)]
    chosen = jax.random.permutation(stream_key, blocks)[partner]
    strong = (owner == chosen) | (owner == (partner + blocks // 2) % blocks)
    return jnp.where(strong, factor * result, result)


def block_scale(stream_key, extent, shards, least, largest):
    level = 1.0
    for position, blocks in shards:
        steps = jax.random.uniform(jax.random.fold_in(jax.random.fold_in(stream_key, 6), position), (blocks,), jnp.float32, least / len(shards), largest / len(shards))
        level = level * jnp.repeat(jnp.exp(steps), extent[position] // blocks).reshape((-1,) + (1,) * (len(extent) - 1 - position))
    return level


def scatter_about(own_key, shape, width, bound, pieces=(), held_as=jnp.bfloat16):
    array = width * jax.random.normal(own_key, shape, jnp.float32)
    if pieces:
        array = array * block_scale(own_key, shape, pieces, -0.22, 0.18)
    return jnp.clip(array, -bound, bound).astype(held_as)


def noise_with(key, extent, scale, most, cuts, heavy, kind=jnp.bfloat16):
    array = scale * jax.random.normal(key, extent, jnp.float32)
    if cuts:
        array = array * block_scale(key, extent, cuts, -0.22, 0.18)
    return jnp.clip(with_spikes(array, jax.random.fold_in(key, 3), *heavy), -most, most).astype(kind)


def setup_inputs(seed: int = 0) -> dict:
    arg_keys = jax.random.split(jax.random.key(seed), 8)
    return {
        "params": scatter_about(arg_keys[0], (REPLICAS, D, FF), D ** -0.5, 0.09375, ((0, 16), (1, 16)), jnp.float32),
        "first_moment": scatter_about(arg_keys[1], (REPLICAS, D, FF), 1.0, 6.0, ((0, 16), (1, 16)), jnp.float32),
        "second_moment": jnp.clip(jnp.exp(math.log(0.5) - 3.218876 * jax.random.uniform(arg_keys[2], (REPLICAS, D, FF), jnp.float32) ** block_scale(arg_keys[2], (REPLICAS, D, FF), ((0, 16), (1, 16)), -0.2, 0.2)), 0.02, 0.5),
        "push_weight": jnp.clip(0.5 + 1.5 * jax.random.uniform(arg_keys[3], (REPLICAS,), jnp.float32) ** block_scale(arg_keys[3], (REPLICAS,), ((0, 16),), -0.2, 0.2), 0.5, 2.0),
        "tokens": noise_with(arg_keys[4], (REPLICAS, TOKENS, D), 1.0, 6.0, ((0, 16), (1, 16)), (1, 2, 16, 2.0)),
        "cotangent": scatter_about(arg_keys[5], (REPLICAS, TOKENS, FF), 0.03, 0.1796875, ((0, 16), (1, 16))),
        "gossip_round": jax.random.randint(arg_keys[6], (1,), 0, REPLICAS).astype(jnp.int32),
    }


beta_one = 0.9
beta_two = 0.999
rate = 0.003
epsilon = 1e-08

def adam_update(param_block, first_block, second_block, gradient):
    correct_one = 1.0 - beta_one ** (STEP_COUNT + 1)
    correct_two = 1.0 - beta_two ** (STEP_COUNT + 1)
    fresh_first = beta_one * first_block + (1.0 - beta_one) * gradient
    fresh_second = beta_two * second_block + (1.0 - beta_two) * (gradient * gradient)
    update = fresh_first / correct_one / (jnp.sqrt(fresh_second / correct_two) + epsilon)
    return (param_block - rate * update, fresh_first, fresh_second)

def replica_step(operands):
    param_block, first_block, second_block, scale_value, token_block, cotangent_block = operands
    weight = (param_block / scale_value).astype(jnp.bfloat16)
    activation = jnp.dot(token_block, weight, preferred_element_type=jnp.float32).astype(jnp.bfloat16)
    gradient = lax.dot_general(token_block, cotangent_block, (((0,), (0,)), ((), ())), preferred_element_type=jnp.float32)
    stepped, fresh_first, fresh_second = adam_update(param_block, first_block, second_block, gradient)
    return (stepped, fresh_first, fresh_second, activation)

def reference(params, first_moment, second_moment, push_weight, tokens, cotangent, gossip_round):
    stepped, fresh_first, fresh_second, activation = lax.map(replica_step, (params, first_moment, second_moment, push_weight, tokens, cotangent))
    levels = REPLICAS.bit_length() - 1
    exponent = (gossip_round[0] % levels).astype(jnp.int32)
    offset = jnp.left_shift(jnp.int32(1), exponent)

    def mixed(values):
        return 0.5 * (values + jnp.roll(values, offset, axis=0))
    return (mixed(stepped), mixed(fresh_first), mixed(fresh_second), mixed(push_weight), activation)
```

```python
import functools

import jax
import jax.numpy as jnp
from jax import lax
from jax.experimental import pallas as pl
from jax.experimental.pallas import tpu as pltpu
from jax.sharding import PartitionSpec as P

STEP_COUNT = 20

beta_one = 0.9
beta_two = 0.999
rate = 0.003
epsilon = 1e-08

MESH = pl.DeviceIdType.MESH
REPLICAS = 16
ROWS = 256
FF = 1024
TOK = 512
QUARTERS = 4
QC = FF // QUARTERS
HALF = QC // 2
F32 = jnp.float32
BF16 = jnp.bfloat16

OPP, NXT, PRV, OWN = 0, 2, 4, 6


def adam(param, first, second):
    correct_one = 1.0 - beta_one ** (STEP_COUNT + 1)
    correct_two = 1.0 - beta_two ** (STEP_COUNT + 1)
    scaled = first * (rate / correct_one)
    return param - scaled / (jnp.sqrt(second * (1.0 / correct_two)) + epsilon)


def kernel(
    offset,
    p_hbm, m_hbm, v_hbm, pw_ref, tok_hbm, cot_hbm,
    np_hbm, nm_hbm, nv_hbm, nw_ref, act_hbm,
    tok_a, tok_b, cot, cot_t, par, mom, sec, par_b, par_r, weights,
    s1_out, s1_in, d_out, d_in, r_out, r_in, r_acc, own_acc, x_out, x_in,
    go_out, go_in, pw_out, pw_in, act_v,
    load_sem, tl_sem, ts_sem, tr_sem, cs_sem,
    wy_s, wy_r, wo_s, wo_r, wx_s, wx_r, wc_s, wc_r,
    s1_s, s1_r, d_s, d_r, r_s, r_r, x_s, x_r,
    gp_sem, gw_sem, go_s, go_r, st_sem, sa_sem,
):
    r = lax.axis_index("replica")
    s = lax.axis_index("shard")
    c = lax.rem(s, 2)
    x = lax.rem(lax.div(s, 2), 2)
    y = lax.div(s, 4)
    ys = [lax.rem(y + 2, 4), lax.rem(y + 1, 4), lax.rem(y + 3, 4), y]

    def at(yy, xx, cc):
        return (r, (yy * 2 + xx) * 2 + cc)

    up, down = at(ys[1], x, c), at(ys[2], x, c)
    across, sibling = at(y, 1 - x, c), at(y, x, 1 - c)
    ahead = (lax.rem(r + offset, REPLICAS), s)
    behind = (lax.rem(r + REPLICAS - offset, REPLICAS), s)

    def remote(src, dst, ss, rs, to):
        return pltpu.make_async_remote_copy(
            src_ref=src, dst_ref=dst, send_sem=ss, recv_sem=rs, device_id=to, device_id_type=MESH
        )

    def columns(i, core):
        block = ys[i // 2] * 2 + (x if i % 2 == 0 else 1 - x)
        return pl.ds(pl.multiple_of((block * 2 + core) * ROWS, ROWS), ROWS)

    def place(i):
        return pl.ds(i * ROWS, ROWS)

    loads = [
        pltpu.make_async_copy(p_hbm, par, load_sem.at[0]),
        pltpu.make_async_copy(cot_hbm, cot.at[0], load_sem.at[1]),
        pltpu.make_async_copy(m_hbm, mom, load_sem.at[2]),
        pltpu.make_async_copy(v_hbm, sec, load_sem.at[3]),
    ]
    load_a = [
        pltpu.make_async_copy(
            tok_hbm.at[:, columns(i, c)], tok_a.at[pl.ds(0, TOK), place(i)], tl_sem.at[i]
        )
        for i in range(8)
    ]
    load_b = [
        pltpu.make_async_copy(
            tok_hbm.at[:, columns(i, 1 - c)], tok_b.at[:, place(i)], tl_sem.at[8 + i]
        )
        for i in range(8)
    ]
    loads[0].start()
    loads[1].start()
    for copy in load_a:
        copy.start()

    barrier = pltpu.get_barrier_semaphore()
    for to in (up, down, across, sibling, ahead, behind):
        pl.semaphore_signal(barrier, inc=1, device_id=to, device_id_type=MESH)
    pl.semaphore_wait(barrier, 6)

    swap_cot = remote(cot_hbm, cot.at[1], cs_sem.at[0], cs_sem.at[1], sibling)
    swap_tok = [
        remote(
            tok_hbm.at[:, columns(i, 1 - c)],
            tok_a.at[pl.ds(TOK, TOK), place(i)],
            ts_sem.at[i], tr_sem.at[i], sibling,
        )
        for i in range(8)
    ]
    swap_cot.start()
    for copy in swap_tok:
        copy.start()

    def w(q, i, parity=0):
        return weights.at[q, parity, place(i), :]

    def w_half(q, i, h):
        return weights.at[q, 0, pl.ds(i * ROWS + h * HALF, HALF), :]

    def send_w_y(q):
        return [
            remote(w(q, OWN), w(q, PRV), wy_s.at[q, 0], wy_r.at[q, 0], up),
            remote(w(q, OWN), w(q, NXT), wy_s.at[q, 1], wy_r.at[q, 1], down),
        ]

    def send_w_opp(q):
        return [
            remote(w_half(q, PRV, 0), w_half(q, OPP, 0), wo_s.at[q, 0], wo_r.at[q, 0], up),
            remote(w_half(q, NXT, 1), w_half(q, OPP, 1), wo_s.at[q, 1], wo_r.at[q, 1], down),
        ]

    def send_w_x(q, i):
        g = i // 2
        return remote(w(q, i), w(q, i + 1), wx_s.at[q, g], wx_r.at[q, g], across)

    def send_w_core(q, i):
        return remote(w(q, i), w(q, i, 1), wc_s.at[q, i], wc_r.at[q, i], sibling)

    def send_s1(q):
        return [
            remote(s1_out.at[q, h], s1_in.at[q, h], s1_s.at[q, h], s1_r.at[q, h], to)
            for h, to in enumerate((up, down))
        ]

    def send_d(q):
        return [
            remote(d_out.at[q, h], d_in.at[q, h], d_s.at[q, h], d_r.at[q, h], to)
            for h, to in enumerate((up, down))
        ]

    def send_r(q):
        return [
            remote(r_out.at[q, h], r_in.at[q, h], r_s.at[q, h], r_r.at[q, h], to)
            for h, to in enumerate((up, down))
        ]

    def send_x(q):
        return remote(x_out.at[q], x_in.at[q], x_s.at[q], x_r.at[q], across)

    send_p = remote(par_b, par_r, gp_sem.at[0], gp_sem.at[1], ahead)
    send_pw = remote(pw_out, pw_in, gw_sem.at[0], gw_sem.at[1], ahead)

    def send_go(q):
        return remote(go_out.at[q], go_in.at[q], go_s.at[q], go_r.at[q], ahead)

    def quarter(q):
        return pl.ds(pl.multiple_of(q * QC, QC), QC)

    def stores(q):
        return [
            pltpu.make_async_copy(src.at[:, quarter(q)], dst.at[:, quarter(q)], st_sem.at[q, n])
            for n, (src, dst) in enumerate(((par, np_hbm), (mom, nm_hbm), (sec, nv_hbm)))
        ]

    def store_act(q):
        return pltpu.make_async_copy(act_v.at[q], act_hbm.at[:, quarter(q)], sa_sem.at[q])

    loads[0].wait()
    par_b[...] = par[...].astype(BF16)
    send_p.start()
    pw_out[...] = jnp.full(pw_out.shape, pw_ref[0], F32)
    send_pw.start()

    @pl.loop(0, QUARTERS)
    def _(q):
        weights[q, 0, place(OWN), :] = (par[:, quarter(q)] / pw_ref[0]).astype(BF16)

    loads[2].start()
    loads[3].start()
    for copy in load_b:
        copy.start()

    def tokens_ready(group):
        for i in (2 * group, 2 * group + 1):
            load_a[i].wait()
            swap_tok[i].wait_recv()

    def product(q, group):
        return jnp.dot(
            cot_t[q], tok_a[:, pl.ds(group * 2 * ROWS, 2 * ROWS)], preferred_element_type=F32
        )

    def issue(q):
        for copy in send_w_y(q):
            copy.start()
        send_w_x(q, OWN).start()
        send_w_core(q, OWN).start()

        @pl.when(q == 0)
        def _():
            loads[1].wait()
            swap_cot.wait_recv()
            tokens_ready(0)

        for n in range(2):
            cot_t[q, :, pl.ds(n * TOK, TOK)] = cot[n, :, quarter(q)].T
        far = product(q, 0)
        s1_out[q, 0] = far[:HALF].astype(BF16)
        s1_out[q, 1] = far[HALF:].astype(BF16)
        for copy in send_s1(q):
            copy.start()

        @pl.when(q == 0)
        def _():
            tokens_ready(1)

        after = product(q, 1)
        d_out[q, 0] = after[HALF:].astype(BF16)
        send_d(q)[0].start()
        r_acc[0] = after[:HALF]

        @pl.when(q == 0)
        def _():
            tokens_ready(2)

        before = product(q, 2)
        d_out[q, 1] = before[:HALF].astype(BF16)
        send_d(q)[1].start()
        r_acc[1] = before[HALF:]

        @pl.when(q == 0)
        def _():
            tokens_ready(3)

        own_acc[lax.rem(q, 2)] = product(q, 3)

    def forward_y(q):
        arrived, onward = send_w_y(q), send_w_opp(q)
        for n, i in ((0, PRV), (1, NXT)):
            arrived[n].wait_recv()
            onward[n].start()
            send_w_x(q, i).start()
            send_w_core(q, i).start()

    def relay(q):
        for n in range(2):
            send_s1(q)[n].wait_recv()
            r_out[q, n] = (r_acc[n] + s1_in[q, n].astype(F32)).astype(BF16)
            send_r(q)[n].start()

    def gather_sum(q):
        slot = lax.rem(q, 2)
        for n in range(2):
            send_d(q)[n].wait_recv()
            send_r(q)[n].wait_recv()
        top = own_acc[slot, :HALF] + r_in[q, 0].astype(F32) + d_in[q, 1].astype(F32)
        low = own_acc[slot, HALF:] + d_in[q, 0].astype(F32) + r_in[q, 1].astype(F32)
        x_out[q, :HALF] = top[:, ROWS:].astype(BF16)
        x_out[q, HALF:] = low[:, ROWS:].astype(BF16)
        send_x(q).start()
        own_acc[slot, :HALF, :ROWS] = top[:, :ROWS]
        own_acc[slot, HALF:, :ROWS] = low[:, :ROWS]

    def forward_opp(q):
        for copy in send_w_opp(q):
            copy.wait_recv()
        send_w_x(q, OPP).start()
        send_w_core(q, OPP).start()

    def update(q):
        @pl.when(q == 0)
        def _():
            loads[2].wait()
            loads[3].wait()

        send_x(q).wait_recv()
        gradient = (own_acc[lax.rem(q, 2), :, :ROWS] + x_in[q].astype(F32)).T
        first = beta_one * mom[:, quarter(q)] + (1.0 - beta_one) * gradient
        second = beta_two * sec[:, quarter(q)] + (1.0 - beta_two) * (gradient * gradient)
        go_out[q, 0] = first.astype(BF16)
        go_out[q, 1] = second.astype(BF16)
        send_go(q).start()
        mom[:, quarter(q)] = first
        sec[:, quarter(q)] = second
        par[:, quarter(q)] = adam(par[:, quarter(q)], first, second)

    def forward_x(q):
        for i in (OWN, PRV, NXT, OPP):
            send_w_x(q, i).wait_recv()
            send_w_core(q, i + 1).start()

    def activation(q):
        @pl.when(q == 0)
        def _():
            for copy in load_b:
                copy.wait()

        for i in range(8):
            send_w_core(q, i).wait_recv()

        @pl.loop(0, 2)
        def _(n):
            rows = pl.ds(pl.multiple_of(n * (TOK // 2), TOK // 2), TOK // 2)
            total = jnp.dot(tok_a[rows, :], weights[q, 0], preferred_element_type=F32)
            total += jnp.dot(tok_b[rows, :], weights[q, 1], preferred_element_type=F32)
            act_v[q, rows, :] = total.astype(BF16)

        store_act(q).start()

    def mix(q):
        @pl.when(q == 0)
        def _():
            send_p.wait_recv()

        send_go(q).wait_recv()
        first = go_in[q, 0].astype(F32)
        second = go_in[q, 1].astype(F32)
        stepped = adam(par_r[:, quarter(q)].astype(F32), first, second)
        par[:, quarter(q)] = 0.5 * (par[:, quarter(q)] + stepped)
        mom[:, quarter(q)] = 0.5 * (mom[:, quarter(q)] + first)
        sec[:, quarter(q)] = 0.5 * (sec[:, quarter(q)] + second)
        for copy in stores(q):
            copy.start()

    def step(t, _):
        @pl.when(jnp.logical_and(t >= 1, t <= 4))
        def _():
            forward_y(t - 1)
            relay(t - 1)

        @pl.when(t <= 3)
        def _():
            issue(t)

        @pl.when(jnp.logical_and(t >= 1, t <= 4))
        def _():
            gather_sum(t - 1)
            forward_opp(t - 1)
            update(t - 1)
            forward_x(t - 1)

        @pl.when(jnp.logical_and(t >= 2, t <= 5))
        def _():
            activation(t - 2)

        @pl.when(t >= 3)
        def _():
            mix(t - 3)

        return 0

    lax.fori_loop(0, 7, step, 0)

    send_pw.wait_recv()
    nw_ref[0] = 0.5 * (pw_ref[0] + pw_in[0, 0])

    swap_cot.wait_send()
    for copy in swap_tok:
        copy.wait_send()
    send_p.wait_send()
    send_pw.wait_send()

    @pl.loop(0, QUARTERS)
    def _(q):
        copies = send_w_y(q) + send_w_opp(q) + send_s1(q) + send_d(q) + send_r(q)
        copies += [send_w_x(q, i) for i in (OPP, NXT, PRV, OWN)]
        copies += [send_w_core(q, i) for i in range(8)]
        copies += [send_x(q), send_go(q)]
        for copy in copies:
            copy.wait_send()
        for copy in stores(q):
            copy.wait()
        store_act(q).wait()


def step_kernel(offset, collective_id):
    any_spec = pl.BlockSpec(memory_space=pl.ANY)
    smem = pl.BlockSpec(memory_space=pltpu.SMEM)
    Q = QUARTERS
    dma = pltpu.SemaphoreType.DMA
    scratch = [
        pltpu.VMEM((2 * TOK, 8 * ROWS), BF16),
        pltpu.VMEM((TOK, 8 * ROWS), BF16),
        pltpu.VMEM((2, TOK, FF), BF16),
        pltpu.VMEM((Q, QC, 2 * TOK), BF16),
        pltpu.VMEM((ROWS, FF), F32),
        pltpu.VMEM((ROWS, FF), F32),
        pltpu.VMEM((ROWS, FF), F32),
        pltpu.VMEM((ROWS, FF), BF16),
        pltpu.VMEM((ROWS, FF), BF16),
        pltpu.VMEM((Q, 2, 8 * ROWS, QC), BF16),
    ]
    scratch += [pltpu.VMEM((Q, 2, HALF, 2 * ROWS), BF16)] * 6
    scratch += [
        pltpu.VMEM((2, HALF, 2 * ROWS), F32),
        pltpu.VMEM((2, QC, 2 * ROWS), F32),
        pltpu.VMEM((Q, QC, ROWS), BF16),
        pltpu.VMEM((Q, QC, ROWS), BF16),
        pltpu.VMEM((Q, 2, ROWS, QC), BF16),
        pltpu.VMEM((Q, 2, ROWS, QC), BF16),
        pltpu.VMEM((8, 128), F32),
        pltpu.VMEM((8, 128), F32),
        pltpu.VMEM((Q, TOK, QC), BF16),
        dma((4,)), dma((16,)), dma((8,)), dma((8,)), dma((2,)),
        dma((Q, 2)), dma((Q, 2)), dma((Q, 2)), dma((Q, 2)),
        dma((Q, 4)), dma((Q, 4)), dma((Q, 8)), dma((Q, 8)),
        dma((Q, 2)), dma((Q, 2)), dma((Q, 2)), dma((Q, 2)), dma((Q, 2)), dma((Q, 2)),
        dma((Q,)), dma((Q,)),
        dma((2,)), dma((2,)), dma((Q,)), dma((Q,)), dma((Q, 3)), dma((Q,)),
    ]
    return pl.pallas_call(
        functools.partial(kernel, offset),
        out_shape=(
            jax.ShapeDtypeStruct((ROWS, FF), F32),
            jax.ShapeDtypeStruct((ROWS, FF), F32),
            jax.ShapeDtypeStruct((ROWS, FF), F32),
            jax.ShapeDtypeStruct((1,), F32),
            jax.ShapeDtypeStruct((TOK, FF), BF16),
        ),
        in_specs=[any_spec, any_spec, any_spec, smem, any_spec, any_spec],
        out_specs=(any_spec, any_spec, any_spec, smem, any_spec),
        scratch_shapes=scratch,
        compiler_params=pltpu.CompilerParams(
            collective_id=collective_id, has_side_effects=True, vmem_limit_bytes=56 << 20
        ),
        name=f"push_step_{offset}",
    )


def per_device(params, first_moment, second_moment, push_weight, tokens, cotangent, gossip_round):
    levels = REPLICAS.bit_length() - 1
    branches = [step_kernel(1 << level, level + 1) for level in range(levels)]
    new_params, new_first, new_second, new_weight, activation = lax.switch(
        gossip_round[0] % levels,
        branches,
        params[0], first_moment[0], second_moment[0], push_weight, tokens[0], cotangent[0],
    )
    return (new_params[None], new_first[None], new_second[None], new_weight, activation[None])


def solution(mesh):
    rows = P("replica", "shard", None)
    return jax.shard_map(
        per_device,
        mesh=mesh,
        in_specs=(rows, rows, rows, P("replica"), rows, rows, P()),
        out_specs=(rows, rows, rows, P("replica"), rows),
        check_vma=False,
    )
```

```python
import functools

import jax
import jax.numpy as jnp
from jax import lax
from jax.experimental import pallas as pl
from jax.experimental.pallas import tpu as pltpu
from jax.sharding import PartitionSpec as P

STEP_COUNT = 20

beta_one = 0.9
beta_two = 0.999
rate = 0.003
epsilon = 1e-08

MESH = pl.DeviceIdType.MESH
REPLICAS = 16
ROWS = 256
FF = 1024
TOK = 512
QUARTERS = 4
QC = FF // QUARTERS
HALF = QC // 2
F32 = jnp.float32
BF16 = jnp.bfloat16

OPP, NXT, PRV, OWN = 0, 2, 4, 6


ORDERS = {
    1: dict(
        activation=(15, 18, 17, 19),
        weights_y=(0, 11, 1, 10),
        issue_far=(8, 4, 3, 1),
        issue_own=(9, 4, 5, 2),
        mix=(19, 13, 16, 8),
        update=(13, 8, 11, 6),
        gather_sum=(9, 7, 8, 3),
        across_own=(12, 6, 9, 13),
        near_y_to_x=(9, -1, -1, -1),
        issue_near=(8, 4, 6, 2),
        across_far=(13, -1, -1, -1),
        far_y=(8, -1, -1, -1),
        near_z=(-1, 14, 13, 15),
        weights_x=(7, 2, 1, 5),
        relay=(8, 5, 7, 2),
        across_to_y=(-1, 8, 9, 13),
        across_near=(14, -1, -1, -1),
        far_both=(-1, 16, 15, 17),
        near_y=(7, 13, 11, 14),
    ),
    2: dict(
        issue_far=(7, 3, 12, 8),
        weights_y=(2, 11, 0, 15),
        gather_sum=(11, 8, 16, 13),
        weights_x=(0, 8, 2, 1),
        near_y=(9, 13, 2, 17),
        across_to_y=(-1, -1, -1, 15),
        across_far=(13, 16, 10, -1),
        far_y=(12, 15, 6, -1),
        across_near=(12, 15, 9, -1),
        across_own=(5, 11, 4, 12),
        near_y_to_x=(9, 13, 2, -1),
        issue_near=(8, 3, 13, 10),
        update=(12, 10, 18, 13),
        near_z=(-1, -1, -1, 18),
        far_both=(-1, -1, -1, 18),
        activation=(13, 16, 10, 18),
        mix=(13, 11, 18, 17),
        issue_own=(10, 5, 14, 8),
        relay=(8, 3, 13, 10),
    ),
    4: dict(
        activation=(19, 8, 17, 18),
        near_z=(-1, -1, -1, 16),
        across_to_y=(-1, -1, -1, 12),
        issue_own=(3, 4, 8, 9),
        far_both=(-1, -1, -1, 17),
        far_y=(17, 7, 13, -1),
        issue_near=(5, 2, 7, 10),
        gather_sum=(7, 5, 8, 12),
        across_far=(18, 7, 14, -1),
        relay=(6, 2, 7, 10),
        weights_x=(7, 0, 3, 1),
        across_near=(17, 7, 16, -1),
        near_y=(14, 4, 10, 15),
        across_own=(15, 2, 9, 7),
        weights_y=(11, 1, 7, 10),
        issue_far=(2, 1, 6, 7),
        update=(7, 6, 11, 13),
        near_y_to_x=(15, 5, 11, -1),
        mix=(12, 11, 16, 19),
        turn_back=(6, -1, -1, -1),
    ),
    8: dict(
        far_both=(-1, -1, -1, 14),
        near_z=(-1, -1, -1, 13),
        across_own=(5, 8, 4, 10),
        far_y=(5, 13, 10, -1),
        across_to_y=(-1, -1, -1, 12),
        weights_x=(0, 3, 1, 6),
        issue_near=(2, 9, 6, 5),
        relay=(2, 9, 7, 5),
        across_far=(7, 14, 11, -1),
        across_near=(7, 14, 10, -1),
        weights_y=(1, 10, 5, 12),
        issue_own=(3, 11, 8, 6),
        activation=(7, 15, 12, 14),
        issue_far=(1, 7, 4, 2),
        gather_sum=(3, 11, 8, 7),
        near_y=(1, 12, 7, 13),
        near_y_to_x=(1, 12, 7, -1),
        mix=(9, 16, 15, 12),
        update=(6, 12, 10, 7),
    ),
}


def adam(param, first, second):
    correct_one = 1.0 - beta_one ** (STEP_COUNT + 1)
    correct_two = 1.0 - beta_two ** (STEP_COUNT + 1)
    scaled = first * (rate / correct_one)
    return param - scaled / (jnp.sqrt(second * (1.0 / correct_two)) + epsilon)


def kernel(
    offset, order,
    p_hbm, m_hbm, v_hbm, pw_ref, tok_hbm, cot_hbm,
    par, mom, sec, nw_ref, act_hbm,
    tok_a, tok_b, cot, cot_t, par_b, par_r, par_relay, weights,
    s1_out, s1_in, d_out, d_in, r_out, r_in, r_acc, own_acc, x_out, x_in,
    go_out, go_in, pw_out, pw_in, act_v,
    load_sem, tl_sem, ts_sem, tr_sem, cs_sem,
    wy_s, wy_r, wo_s, wo_r, wz_s, wz_r, wq_s, wq_r, wx_s, wx_r, wc_s, wc_r,
    s1_s, s1_r, d_s, d_r, r_s, r_r, x_s, x_r,
    gp_sem, gw_sem, go_s, go_r, sa_sem,
):
    r = lax.axis_index("replica")
    s = lax.axis_index("shard")
    c = lax.rem(s, 2)
    x = lax.rem(lax.div(s, 2), 2)
    y = lax.div(s, 4)
    ys = [lax.rem(y + 2, 4), lax.rem(y + 1, 4), lax.rem(y + 3, 4), y]

    def at(yy, xx, cc):
        return (r, (yy * 2 + xx) * 2 + cc)

    up, down = at(ys[1], x, c), at(ys[2], x, c)
    across, sibling = at(y, 1 - x, c), at(y, x, 1 - c)
    ahead = (lax.rem(r + offset, REPLICAS), s)
    behind = (lax.rem(r + REPLICAS - offset, REPLICAS), s)

    def remote(src, dst, ss, rs, to):
        return pltpu.make_async_remote_copy(
            src_ref=src, dst_ref=dst, send_sem=ss, recv_sem=rs, device_id=to, device_id_type=MESH
        )

    def columns(i, core):
        block = ys[i // 2] * 2 + (x if i % 2 == 0 else 1 - x)
        return pl.ds(pl.multiple_of((block * 2 + core) * ROWS, ROWS), ROWS)

    def place(i):
        return pl.ds(i * ROWS, ROWS)

    loads = [
        pltpu.make_async_copy(p_hbm, par, load_sem.at[0]),
        pltpu.make_async_copy(cot_hbm, cot.at[0], load_sem.at[1]),
        pltpu.make_async_copy(m_hbm, mom, load_sem.at[2]),
        pltpu.make_async_copy(v_hbm, sec, load_sem.at[3]),
    ]
    load_a = [
        pltpu.make_async_copy(
            tok_hbm.at[:, columns(i, c)], tok_a.at[pl.ds(0, TOK), place(i)], tl_sem.at[i]
        )
        for i in range(8)
    ]
    load_b = [
        pltpu.make_async_copy(
            tok_hbm.at[:, columns(i, 1 - c)], tok_b.at[:, place(i)], tl_sem.at[8 + i]
        )
        for i in range(8)
    ]
    loads[0].start()
    loads[1].start()
    for copy in load_a:
        copy.start()

    barrier = pltpu.get_barrier_semaphore()
    partners = [up, down, across, sibling, ahead, behind]
    back = (lax.rem(r + REPLICAS - 6, REPLICAS), s)
    if offset == 4:
        partners += [back, (lax.rem(r + 6, REPLICAS), s)]
    for to in partners:
        pl.semaphore_signal(barrier, inc=1, device_id=to, device_id_type=MESH)
    pl.semaphore_wait(barrier, len(partners))

    def quarter(q):
        return pl.ds(pl.multiple_of(q * QC, QC), QC)

    def swap_cot(q):
        return remote(
            cot_hbm.at[:, quarter(q)], cot.at[1, :, quarter(q)],
            ts_sem.at[1], cs_sem.at[q], sibling,
        )

    swap_tok = [
        remote(
            tok_hbm.at[:, columns(i, 1 - c)],
            tok_a.at[pl.ds(TOK, TOK), place(i)],
            ts_sem.at[0], tr_sem.at[i], sibling,
        )
        for i in range(8)
    ]
    turns = sorted(range(QUARTERS), key=lambda q: order["issue_far"][q])
    swap_cot(turns[0]).start()
    for copy in swap_tok:
        copy.start()
    for q in turns[1:]:
        swap_cot(q).start()

    def w(q, i, parity=0):
        return weights.at[q, parity, place(i), :]

    def w_half(q, i, h):
        return weights.at[q, 0, pl.ds(i * ROWS + h * HALF, HALF), :]

    def send_w_y(q):
        return [
            remote(w(q, OWN), w(q, PRV), wy_s.at[0], wy_r.at[q, 0], up),
            remote(w(q, OWN), w(q, NXT), wy_s.at[0], wy_r.at[q, 1], down),
        ]

    def send_w_opp(q):
        return [
            remote(w_half(q, PRV, 0), w_half(q, OPP, 0), wo_s.at[0], wo_r.at[q, 0], up),
            remote(w_half(q, NXT, 1), w_half(q, OPP, 1), wo_s.at[0], wo_r.at[q, 1], down),
        ]

    def send_w_z(q):
        return [
            remote(w(q, OWN + 1), w(q, PRV + 1), wz_s.at[0], wz_r.at[q, 0], up),
            remote(w(q, OWN + 1), w(q, NXT + 1), wz_s.at[0], wz_r.at[q, 1], down),
        ]

    def send_w_far(q):
        return [
            remote(
                w_half(q, PRV + 1, 0), w_half(q, OPP + 1, 0), wq_s.at[0], wq_r.at[q, 0], up
            ),
            remote(
                w_half(q, NXT + 1, 1), w_half(q, OPP + 1, 1), wq_s.at[0], wq_r.at[q, 1], down
            ),
        ]

    def send_w_x(q, i):
        g = i // 2
        return remote(w(q, i), w(q, i + 1), wx_s.at[0], wx_r.at[q, g], across)

    def send_w_core(q, i):
        return remote(w(q, i), w(q, i, 1), wc_s.at[0], wc_r.at[q, i], sibling)

    def send_s1(q):
        return [
            remote(s1_out.at[q, h], s1_in.at[q, h], s1_s.at[0], s1_r.at[q, h], to)
            for h, to in enumerate((up, down))
        ]

    def send_d(q):
        return [
            remote(d_out.at[q, h], d_in.at[q, h], d_s.at[0], d_r.at[q, h], to)
            for h, to in enumerate((up, down))
        ]

    def send_r(q):
        return [
            remote(r_out.at[q, h], r_in.at[q, h], r_s.at[0], r_r.at[q, h], to)
            for h, to in enumerate((up, down))
        ]

    def send_x(q):
        return remote(x_out.at[q], x_in.at[q], x_s.at[0], x_r.at[q], across)

    two_ways = offset == 4
    near_half, far_half = pl.ds(0, ROWS // 2), pl.ds(ROWS // 2, ROWS // 2)
    if two_ways:
        send_p = remote(
            par_b.at[near_half], par_r.at[near_half], gp_sem.at[0], gp_sem.at[1], ahead
        )
        leg_one = remote(par_b.at[far_half], par_relay, gp_sem.at[2], gp_sem.at[3], back)
        leg_two = remote(par_relay, par_r.at[far_half], gp_sem.at[4], gp_sem.at[5], back)
    else:
        send_p = remote(par_b, par_r, gp_sem.at[0], gp_sem.at[1], ahead)
    send_pw = remote(pw_out, pw_in, gw_sem.at[0], gw_sem.at[1], ahead)

    def send_go(q):
        return remote(go_out.at[q], go_in.at[q], go_s.at[0], go_r.at[q], ahead)

    loads[0].wait()
    par_b[...] = par[...].astype(BF16)
    if two_ways:
        leg_one.start()
    send_p.start()
    pw_out[...] = jnp.full(pw_out.shape, pw_ref[0], F32)
    send_pw.start()

    @pl.loop(0, QUARTERS)
    def _(q):
        weights[q, 0, place(OWN), :] = (par[:, quarter(q)] / pw_ref[0]).astype(BF16)

    loads[2].start()
    loads[3].start()
    for copy in load_b:
        copy.start()

    def tokens_ready(group):
        for i in (2 * group, 2 * group + 1):
            load_a[i].wait()
            swap_tok[i].wait_recv()

    def product(q, group):
        return jnp.dot(
            cot_t[q], tok_a[:, pl.ds(group * 2 * ROWS, 2 * ROWS)], preferred_element_type=F32
        )

    def weights_y(q, first):
        for copy in send_w_y(q):
            copy.start()

    def weights_x(q, first):
        send_w_x(q, OWN).start()

    def issue_far(q, first):
        @pl.when(first)
        def _():
            loads[1].wait()
            tokens_ready(0)

        swap_cot(q).wait_recv()
        for n in range(2):
            cot_t[q, :, pl.ds(n * TOK, TOK)] = cot[n, :, quarter(q)].T
        far = product(q, 0)
        s1_out[q, 0] = far[:HALF].astype(BF16)
        s1_out[q, 1] = far[HALF:].astype(BF16)
        for copy in send_s1(q):
            copy.start()

    def issue_near(q, first):
        @pl.when(first)
        def _():
            tokens_ready(1)

        after = product(q, 1)
        d_out[q, 0] = after[HALF:].astype(BF16)
        send_d(q)[0].start()
        r_acc[q, 0] = after[:HALF]

        @pl.when(first)
        def _():
            tokens_ready(2)

        before = product(q, 2)
        d_out[q, 1] = before[:HALF].astype(BF16)
        send_d(q)[1].start()
        r_acc[q, 1] = before[HALF:]

    def issue_own(q, first):
        @pl.when(first)
        def _():
            tokens_ready(3)

        own_acc[q] = product(q, 3)

    def relay(q, first):
        for n in range(2):
            send_s1(q)[n].wait_recv()
            r_out[q, n] = (r_acc[q, n] + s1_in[q, n].astype(F32)).astype(BF16)
            send_r(q)[n].start()

    def gather_sum(q, first):
        for n in range(2):
            send_d(q)[n].wait_recv()
            send_r(q)[n].wait_recv()
        top = own_acc[q, :HALF] + r_in[q, 0].astype(F32) + d_in[q, 1].astype(F32)
        low = own_acc[q, HALF:] + d_in[q, 0].astype(F32) + r_in[q, 1].astype(F32)
        x_out[q, :HALF] = top[:, ROWS:].astype(BF16)
        x_out[q, HALF:] = low[:, ROWS:].astype(BF16)
        send_x(q).start()
        own_acc[q, :HALF, :ROWS] = top[:, :ROWS]
        own_acc[q, HALF:, :ROWS] = low[:, :ROWS]

    def update(q, first):
        @pl.when(first)
        def _():
            loads[2].wait()
            loads[3].wait()

        send_x(q).wait_recv()
        gradient = (own_acc[q, :, :ROWS] + x_in[q].astype(F32)).T
        fresh = beta_one * mom[:, quarter(q)] + (1.0 - beta_one) * gradient
        second = beta_two * sec[:, quarter(q)] + (1.0 - beta_two) * (gradient * gradient)
        go_out[q, 0] = fresh.astype(BF16)
        go_out[q, 1] = second.astype(BF16)
        send_go(q).start()
        mom[:, quarter(q)] = fresh
        sec[:, quarter(q)] = second
        par[:, quarter(q)] = adam(par[:, quarter(q)], fresh, second)

    def near_y(q, first):
        arrived, onward = send_w_y(q), send_w_opp(q)
        for n, i in ((0, PRV), (1, NXT)):
            arrived[n].wait_recv()
            onward[n].start()
            send_w_core(q, i).start()

    def near_y_to_x(q, first):
        send_w_x(q, PRV).start()
        send_w_x(q, NXT).start()

    def across_own(q, first):
        send_w_x(q, OWN).wait_recv()
        send_w_core(q, OWN + 1).start()

    def across_to_y(q, first):
        for copy in send_w_z(q):
            copy.start()

    def far_y(q, first):
        for copy in send_w_opp(q):
            copy.wait_recv()
        send_w_x(q, OPP).start()
        send_w_core(q, OPP).start()

    def across_near(q, first):
        for i in (PRV, NXT):
            send_w_x(q, i).wait_recv()
            send_w_core(q, i + 1).start()

    def across_far(q, first):
        send_w_x(q, OPP).wait_recv()
        send_w_core(q, OPP + 1).start()

    def near_z(q, first):
        arrived, onward = send_w_z(q), send_w_far(q)
        for n, i in ((0, PRV + 1), (1, NXT + 1)):
            arrived[n].wait_recv()
            onward[n].start()
            send_w_core(q, i).start()

    def far_both(q, first):
        for copy in send_w_opp(q):
            copy.wait_recv()
        send_w_core(q, OPP).start()
        for copy in send_w_far(q):
            copy.wait_recv()
        send_w_core(q, OPP + 1).start()

    def activation(q, first):
        @pl.when(first)
        def _():
            for copy in load_b:
                copy.wait()

        for i in range(8):
            send_w_core(q, i).wait_recv()

        @pl.loop(0, 2)
        def _(n):
            rows = pl.ds(pl.multiple_of(n * (TOK // 2), TOK // 2), TOK // 2)
            total = jnp.dot(tok_a[rows, :], weights[q, 0], preferred_element_type=F32)
            total += jnp.dot(tok_b[rows, :], weights[q, 1], preferred_element_type=F32)
            act_v[q, rows, :] = total.astype(BF16)

        store_act(q).start()

    def store_act(q):
        return pltpu.make_async_copy(act_v.at[q], act_hbm.at[:, quarter(q)], sa_sem.at[q])

    def turn_back(q, first):
        leg_one.wait_recv()
        leg_two.start()

    def mix(q, first):
        @pl.when(first)
        def _():
            send_p.wait_recv()
            if two_ways:
                leg_two.wait_recv()

        send_go(q).wait_recv()
        theirs = go_in[q, 0].astype(F32)
        second = go_in[q, 1].astype(F32)
        stepped = adam(par_r[:, quarter(q)].astype(F32), theirs, second)
        par[:, quarter(q)] = 0.5 * (par[:, quarter(q)] + stepped)
        mom[:, quarter(q)] = 0.5 * (mom[:, quarter(q)] + theirs)
        sec[:, quarter(q)] = 0.5 * (sec[:, quarter(q)] + second)

    events = {
        event.__name__: event
        for event in (
            weights_y, weights_x, issue_far, issue_near, issue_own, relay, gather_sum, update,
            near_y, near_y_to_x, across_own, across_to_y, far_y, across_near, across_far,
            near_z, far_both, activation, mix, turn_back,
        )
    }
    for n in turns:
        send_w_core(n, OWN).start()

    def run(i, _):
        for name, places in order.items():
            places = {q: n for q, n in enumerate(places) if n >= 0}
            here, q = False, 0
            for turn, n in places.items():
                here = jnp.logical_or(here, i == n)
                q = q + turn * (i == n).astype(jnp.int32)
            event = events[name]

            @pl.when(here)
            def _():
                event(q, i == min(places.values()))

        return 0

    passes = 1 + max(max(places) for places in order.values())
    lax.fori_loop(0, passes, run, 0)

    send_pw.wait_recv()
    nw_ref[0] = 0.5 * (pw_ref[0] + pw_in[0, 0])

    def sent(ref, sem):
        pltpu.make_async_copy(ref, ref, sem).wait()

    def finish():
        across = sum(4 if order["near_y_to_x"][q] >= 0 else 1 for q in range(QUARTERS))
        around = QUARTERS if "across_to_y" not in order else sum(
            n < 0 for n in order["across_to_y"]
        )
        around = QUARTERS - around
        sent(tok_a.at[pl.ds(TOK, TOK)], ts_sem.at[0])
        sent(cot.at[1], ts_sem.at[1])
        sent(weights.at[:, 0], wc_s.at[0])
        sent(weights.at[0, 0], wy_s.at[0])
        sent(weights.at[0, 0, pl.ds(0, 4 * ROWS)], wo_s.at[0])
        if around:
            sent(weights.at[0, 0, pl.ds(0, 2 * around * ROWS)], wz_s.at[0])
            sent(weights.at[0, 0, pl.ds(0, around * ROWS)], wq_s.at[0])
        sent(tok_b.at[pl.ds(0, across * (TOK // 16))], wx_s.at[0])
        sent(s1_out, s1_s.at[0])
        sent(d_out, d_s.at[0])
        sent(r_out, r_s.at[0])
        sent(x_out, x_s.at[0])
        sent(go_out, go_s.at[0])
        send_p.wait_send()
        send_pw.wait_send()
        for q in range(QUARTERS):
            store_act(q).wait()
        if two_ways:
            leg_one.wait_send()
            leg_two.wait_send()

    finish()


def leave_kernel(*refs):
    states, act, new_states, new_act, held, sems = refs[:3], refs[3], refs[4:7], refs[7], *refs[8:]
    blocks = [pl.ds(n * TOK // 4, TOK // 4) for n in range(4)]
    loads = [
        pltpu.make_async_copy(act.at[rows], held.at[rows], sems.at[n])
        for n, rows in enumerate(blocks)
    ]
    copies = [
        pltpu.make_async_copy(src, dst, sems.at[4 + n])
        for n, (src, dst) in enumerate(zip(states, new_states))
    ]
    stores = [
        pltpu.make_async_copy(held.at[rows], new_act.at[rows], sems.at[7 + n])
        for n, rows in enumerate(blocks)
    ]
    for copy in loads + copies:
        copy.start()
    for load, store in zip(loads, stores):
        load.wait()
        store.start()
    for copy in copies + stores:
        copy.wait()


def leave(states, activation):
    arrays = [pltpu.with_memory_space_constraint(a, pltpu.VMEM) for a in states] + [activation]
    return pl.pallas_call(
        leave_kernel,
        out_shape=tuple(jax.ShapeDtypeStruct(a.shape, a.dtype) for a in arrays),
        in_specs=[pl.BlockSpec(memory_space=pltpu.VMEM)] * len(states)
        + [pl.BlockSpec(memory_space=pl.ANY)],
        out_specs=tuple(pl.BlockSpec(memory_space=pl.ANY) for _ in arrays),
        scratch_shapes=[pltpu.VMEM((TOK, FF), BF16), pltpu.SemaphoreType.DMA((11,))],
        compiler_params=pltpu.CompilerParams(vmem_limit_bytes=8 << 20),
        name="leave",
    )(*arrays)


def step_kernel(offset, collective_id):
    any_spec = pl.BlockSpec(memory_space=pl.ANY)
    smem = pl.BlockSpec(memory_space=pltpu.SMEM)
    vmem = pl.BlockSpec(memory_space=pltpu.VMEM)
    Q = QUARTERS
    dma = pltpu.SemaphoreType.DMA
    scratch = [
        pltpu.VMEM((2 * TOK, 8 * ROWS), BF16),
        pltpu.VMEM((TOK, 8 * ROWS), BF16),
        pltpu.VMEM((2, TOK, FF), BF16),
        pltpu.VMEM((Q, QC, 2 * TOK), BF16),
        pltpu.VMEM((ROWS, FF), BF16),
        pltpu.VMEM((ROWS, FF), BF16),
        pltpu.VMEM((ROWS // 2, FF), BF16),
        pltpu.VMEM((Q, 2, 8 * ROWS, QC), BF16),
    ]
    scratch += [pltpu.VMEM((Q, 2, HALF, 2 * ROWS), BF16)] * 6
    scratch += [
        pltpu.VMEM((Q, 2, HALF, 2 * ROWS), F32),
        pltpu.VMEM((Q, QC, 2 * ROWS), F32),
        pltpu.VMEM((Q, QC, ROWS), BF16),
        pltpu.VMEM((Q, QC, ROWS), BF16),
        pltpu.VMEM((Q, 2, ROWS, QC), BF16),
        pltpu.VMEM((Q, 2, ROWS, QC), BF16),
        pltpu.VMEM((8, 128), F32),
        pltpu.VMEM((8, 128), F32),
        pltpu.VMEM((Q, TOK, QC), BF16),
        dma((4,)), dma((16,)), dma((2,)), dma((8,)), dma((Q,)),
        dma((1,)), dma((Q, 2)), dma((1,)), dma((Q, 2)),
        dma((1,)), dma((Q, 2)), dma((1,)), dma((Q, 2)),
        dma((1,)), dma((Q, 4)), dma((1,)), dma((Q, 8)),
        dma((1,)), dma((Q, 2)), dma((1,)), dma((Q, 2)), dma((1,)), dma((Q, 2)),
        dma((1,)), dma((Q,)),
        dma((6,)), dma((2,)), dma((1,)), dma((Q,)), dma((Q,)),
    ]
    return pl.pallas_call(
        functools.partial(kernel, offset, ORDERS[offset]),
        out_shape=(
            pltpu.VMEM((ROWS, FF), F32),
            pltpu.VMEM((ROWS, FF), F32),
            pltpu.VMEM((ROWS, FF), F32),
            jax.ShapeDtypeStruct((1,), F32),
            jax.ShapeDtypeStruct((TOK, FF), BF16),
        ),
        in_specs=[any_spec, any_spec, any_spec, smem, any_spec, any_spec],
        out_specs=(vmem, vmem, vmem, smem, any_spec),
        scratch_shapes=scratch,
        compiler_params=pltpu.CompilerParams(
            collective_id=collective_id, has_side_effects=True, vmem_limit_bytes=48 << 20
        ),
        name=f"push_step_{offset}",
    )


def per_device(params, first_moment, second_moment, push_weight, tokens, cotangent, gossip_round):
    levels = REPLICAS.bit_length() - 1
    branches = [step_kernel(1 << level, level + 1) for level in range(levels)]
    new_params, new_first, new_second, new_weight, activation = lax.switch(
        gossip_round[0] % levels,
        branches,
        params[0], first_moment[0], second_moment[0], push_weight, tokens[0], cotangent[0],
    )
    new_params, new_first, new_second, activation = leave(
        (new_params, new_first, new_second), activation
    )
    return (new_params[None], new_first[None], new_second[None], new_weight, activation[None])


def solution(mesh):
    rows = P("replica", "shard", None)
    return jax.shard_map(
        per_device,
        mesh=mesh,
        in_specs=(rows, rows, rows, P("replica"), rows, rows, P()),
        out_specs=(rows, rows, rows, P("replica"), rows),
        check_vma=False,
    )
```

```python
import functools

import jax
import jax.numpy as jnp
from jax import lax
from jax.experimental import pallas as pl
from jax.experimental.pallas import tpu as pltpu
from jax.sharding import PartitionSpec as P

STEP_COUNT = 20

beta_one = 0.9
beta_two = 0.999
rate = 0.003
epsilon = 1e-08

MESH = pl.DeviceIdType.MESH
REPLICAS = 16
ROWS = 256
FF = 1024
TOK = 512
QUARTERS = 4
QC = FF // QUARTERS
HALF = QC // 2
F32 = jnp.float32
BF16 = jnp.bfloat16

OPP, NXT, PRV, OWN = 0, 2, 4, 6


ORDERS = {
    1: dict(
        across_far=(24, -1, -1, -1),
        across_own=(21, 3, 7, 12),
        weights_y=(2, 13, 12, 20),
        gather_sum=(15, 8, 10, 14),
        issue_far=(8, 2, 4, 7),
        params_x=(5, 3, 9, 6),
        weights_x=(20, 1, 0, 2),
        near_y_to_x=(20, -1, -1, -1),
        across_to_y=(-1, 15, 13, 16),
        update=(17, 10, 11, 16),
        near_z=(-1, 19, 20, 21),
        activation_most=(24, 20, 22, 23),
        across_near=(23, -1, -1, -1),
        activation_rest=(25, 21, 23, 24),
        far_y=(20, -1, -1, -1),
        pass_on=(20, 13, 14, 18),
        issue_near=(11, 2, 5, 10),
        relay=(11, 4, 6, 10),
        issue_own=(8, 3, 6, 9),
        mix=(25, 17, 18, 21),
        near_y=(11, 19, 20, 21),
        far_both=(-1, 20, 22, 23),
    ),
    2: dict(
        activation_most=(11, 20, 13, 21),
        across_near=(10, 19, 9, -1),
        far_y=(5, 19, 10, -1),
        near_z=(-1, -1, -1, 20),
        relay=(10, 15, 4, 12),
        near_y=(3, 16, 4, 19),
        near_y_to_x=(3, 16, 4, -1),
        issue_far=(5, 13, 3, 7),
        across_far=(10, 20, 13, -1),
        gather_sum=(13, 17, 8, 14),
        weights_x=(1, 10, 2, 14),
        issue_near=(9, 14, 3, 10),
        activation_rest=(12, 20, 13, 21),
        issue_own=(8, 13, 3, 7),
        update=(13, 19, 11, 15),
        weights_y=(0, 13, 2, 16),
        mix=(18, 21, 13, 17),
        far_both=(-1, -1, -1, 20),
        across_own=(5, 15, 6, 18),
        across_to_y=(-1, -1, -1, 18),
    ),
    4: dict(
        issue_near=(6, 2, 10, 5),
        issue_own=(6, 2, 9, 4),
        weights_x=(1, 0, 2, 3),
        relay=(7, 2, 10, 5),
        far_both=(-1, -1, -1, 17),
        weights_y=(12, 0, 9, 11),
        across_to_y=(-1, -1, -1, 14),
        across_near=(17, 7, 16, -1),
        far_y=(16, 7, 15, -1),
        near_y=(15, 3, 10, 14),
        issue_far=(5, 1, 8, 2),
        near_y_to_x=(15, 5, 10, -1),
        update=(11, 5, 14, 7),
        across_far=(19, 9, 16, -1),
        activation_most=(19, 8, 17, 16),
        across_own=(12, 2, 10, 6),
        near_z=(-1, -1, -1, 15),
        turn_back=(5, -1, -1, -1),
        gather_sum=(9, 3, 13, 6),
        activation_rest=(19, 9, 17, 18),
        mix=(15, 12, 19, 13),
    ),
    8: dict(
        activation_rest=(8, 18, 16, 17),
        issue_own=(10, 4, 2, 8),
        near_y_to_x=(3, 15, 10, -1),
        far_both=(-1, -1, -1, 16),
        across_own=(6, 8, 9, 3),
        issue_near=(8, 3, 1, 5),
        weights_x=(1, 6, 7, 0),
        gather_sum=(11, 6, 3, 9),
        across_far=(6, 17, 14, -1),
        far_y=(5, 16, 13, -1),
        across_near=(6, 16, 12, -1),
        across_to_y=(-1, -1, -1, 13),
        activation_most=(7, 17, 13, 16),
        relay=(10, 3, 2, 6),
        update=(13, 9, 5, 10),
        mix=(18, 13, 10, 16),
        weights_y=(0, 10, 6, 11),
        issue_far=(7, 2, 0, 4),
        near_y=(2, 14, 9, 15),
        near_z=(-1, -1, -1, 15),
    ),
}


def adam(param, first, second):
    correct_one = 1.0 - beta_one ** (STEP_COUNT + 1)
    correct_two = 1.0 - beta_two ** (STEP_COUNT + 1)
    scaled = first * (rate / correct_one)
    return param - scaled / (jnp.sqrt(second * (1.0 / correct_two)) + epsilon)


def kernel(
    offset, order,
    p_hbm, m_hbm, v_hbm, pw_ref, tok_hbm, cot_hbm,
    par, mom, sec, nw_hbm, act_hbm,
    tok_a, tok_b, cot, cot_t, par_b, par_r, par_relay, weights,
    s1_out, s1_in, d_out, d_in, r_out, r_in, r_acc, own_acc, x_out, x_in,
    go_out, go_in, go_relay, pw_out, pw_in, nw_ref, act_acc, act_v,
    load_sem, tl_sem, ts_sem, tr_sem, cs_sem,
    wy_s, wy_r, wo_s, wo_r, wz_s, wz_r, wq_s, wq_r, wx_s, wx_r, wc_s, wc_r,
    s1_s, s1_r, d_s, d_r, r_s, r_r, x_s, x_r,
    gp_sem, gw_sem, go_s, go_r, gl_s, gl_r, gq_s, gq_r, sa_sem, nw_sem,
):
    r = lax.axis_index("replica")
    s = lax.axis_index("shard")
    c = lax.rem(s, 2)
    x = lax.rem(lax.div(s, 2), 2)
    y = lax.div(s, 4)
    ys = [lax.rem(y + 2, 4), lax.rem(y + 1, 4), lax.rem(y + 3, 4), y]

    def at(yy, xx, cc):
        return (r, (yy * 2 + xx) * 2 + cc)

    up, down = at(ys[1], x, c), at(ys[2], x, c)
    across, sibling = at(y, 1 - x, c), at(y, x, 1 - c)
    two_legs = offset == 1
    peer = s if not two_legs else at(y, 1 - x, c)[1]
    ahead = (lax.rem(r + offset, REPLICAS), peer)
    behind = (lax.rem(r + REPLICAS - offset, REPLICAS), peer)

    def remote(src, dst, ss, rs, to):
        return pltpu.make_async_remote_copy(
            src_ref=src, dst_ref=dst, send_sem=ss, recv_sem=rs, device_id=to, device_id_type=MESH
        )

    def columns(i, core):
        block = ys[i // 2] * 2 + (x if i % 2 == 0 else 1 - x)
        return pl.ds(pl.multiple_of((block * 2 + core) * ROWS, ROWS), ROWS)

    def place(i):
        return pl.ds(i * ROWS, ROWS)

    loads = [
        pltpu.make_async_copy(p_hbm, par, load_sem.at[0]),
        pltpu.make_async_copy(cot_hbm, cot.at[0], load_sem.at[1]),
        pltpu.make_async_copy(m_hbm, mom, load_sem.at[2]),
        pltpu.make_async_copy(v_hbm, sec, load_sem.at[3]),
    ]
    load_a = [
        pltpu.make_async_copy(
            tok_hbm.at[:, columns(i, c)], tok_a.at[pl.ds(0, TOK), place(i)], tl_sem.at[i // 2]
        )
        for i in range(8)
    ]
    load_b = [
        pltpu.make_async_copy(
            tok_hbm.at[:, columns(i, 1 - c)], tok_b.at[:, place(i)], tl_sem.at[4]
        )
        for i in range(8)
    ]
    loads[0].start()
    loads[1].start()
    for copy in load_a:
        copy.start()

    barrier = pltpu.get_barrier_semaphore()
    partners = [up, down, across, sibling, ahead, behind]
    back = (lax.rem(r + REPLICAS - 6, REPLICAS), s)
    if offset == 4:
        partners += [back, (lax.rem(r + 6, REPLICAS), s)]
    for to in partners:
        pl.semaphore_signal(barrier, inc=1, device_id=to, device_id_type=MESH)
    pl.semaphore_wait(barrier, len(partners))

    def quarter(q):
        return pl.ds(pl.multiple_of(q * QC, QC), QC)

    def swap_cot(q):
        return remote(
            cot_hbm.at[:, quarter(q)], cot.at[1, :, quarter(q)],
            ts_sem.at[1], cs_sem.at[q], sibling,
        )

    swap_tok = [
        remote(
            tok_hbm.at[:, columns(i, 1 - c)],
            tok_a.at[pl.ds(TOK, TOK), place(i)],
            ts_sem.at[0], tr_sem.at[i // 2], sibling,
        )
        for i in range(8)
    ]
    turns = sorted(range(QUARTERS), key=lambda q: order["issue_far"][q])
    swap_cot(turns[0]).start()
    for copy in swap_tok:
        copy.start()
    for q in turns[1:]:
        swap_cot(q).start()

    def w(q, i, parity=0):
        return weights.at[q, parity, place(i), :]

    def w_half(q, i, h):
        return weights.at[q, 0, pl.ds(i * ROWS + h * HALF, HALF), :]

    def send_w_y(q):
        return [
            remote(w(q, OWN), w(q, PRV), wy_s.at[0], wy_r.at[q], up),
            remote(w(q, OWN), w(q, NXT), wy_s.at[0], wy_r.at[q], down),
        ]

    def send_w_opp(q):
        return [
            remote(w_half(q, PRV, 0), w_half(q, OPP, 0), wo_s.at[0], wo_r.at[q], up),
            remote(w_half(q, NXT, 1), w_half(q, OPP, 1), wo_s.at[0], wo_r.at[q], down),
        ]

    def send_w_z(q):
        return [
            remote(w(q, OWN + 1), w(q, PRV + 1), wz_s.at[0], wz_r.at[q], up),
            remote(w(q, OWN + 1), w(q, NXT + 1), wz_s.at[0], wz_r.at[q], down),
        ]

    def send_w_far(q):
        return [
            remote(
                w_half(q, PRV + 1, 0), w_half(q, OPP + 1, 0), wq_s.at[0], wq_r.at[q], up
            ),
            remote(
                w_half(q, NXT + 1, 1), w_half(q, OPP + 1, 1), wq_s.at[0], wq_r.at[q], down
            ),
        ]

    def send_w_x(q, i):
        g = i // 2
        return remote(w(q, i), w(q, i + 1), wx_s.at[0], wx_r.at[q, g], across)

    def send_w_core(q, i):
        return remote(w(q, i), w(q, i, 1), wc_s.at[0], wc_r.at[q, min(i // 2, 1)], sibling)

    def send_s1(q):
        return [
            remote(s1_out.at[q, h], s1_in.at[q, h], s1_s.at[0], s1_r.at[q], to)
            for h, to in enumerate((up, down))
        ]

    def send_d(q):
        return [
            remote(d_out.at[q, h], d_in.at[q, h], d_s.at[0], d_r.at[q], to)
            for h, to in enumerate((up, down))
        ]

    def send_r(q):
        return [
            remote(r_out.at[q, h], r_in.at[q, h], r_s.at[0], r_r.at[q], to)
            for h, to in enumerate((up, down))
        ]

    def send_x(q):
        return remote(x_out.at[q], x_in.at[q], x_s.at[0], x_r.at[q], across)

    two_ways = offset == 4
    near_half, far_half = pl.ds(0, ROWS // 2), pl.ds(ROWS // 2, ROWS // 2)
    if two_ways:
        send_p = remote(
            par_b.at[near_half], par_r.at[near_half], gp_sem.at[0], gp_sem.at[1], ahead
        )
        leg_one = remote(par_b.at[far_half], par_relay, gp_sem.at[2], gp_sem.at[3], back)
        leg_two = remote(par_relay, par_r.at[far_half], gp_sem.at[4], gp_sem.at[5], back)
    else:
        send_p = remote(par_b, par_r, gp_sem.at[0], gp_sem.at[1], ahead)
    send_pw = remote(pw_out, pw_in, gw_sem.at[0], gw_sem.at[1], ahead)

    def send_go(q):
        source = go_relay if two_legs else go_out
        return remote(source.at[q], go_in.at[q], go_s.at[0], go_r.at[q], ahead)

    states = pl.ds(0, 2)

    def leg_states(q):
        return remote(
            go_out.at[q], go_relay.at[q, states], gl_s.at[0], gl_r.at[q], across
        )

    def leg_params(q):
        return remote(
            par_b.at[:, quarter(q)], go_relay.at[q, 2], gq_s.at[0], gq_r.at[q], across
        )

    loads[0].wait()
    par_b[...] = par[...].astype(BF16)
    if two_ways:
        leg_one.start()
    if not two_legs:
        send_p.start()
    pw_out[...] = jnp.full(pw_out.shape, pw_ref[0], F32)
    send_pw.start()

    @pl.loop(0, QUARTERS)
    def _(q):
        weights[q, 0, place(OWN), :] = (par[:, quarter(q)] / pw_ref[0]).astype(BF16)

    loads[2].start()
    loads[3].start()
    for copy in load_b:
        copy.start()

    def ended(ref, sem):
        pltpu.make_async_copy(ref, ref, sem).wait()

    def tokens_ready(group):
        pair = pl.ds(group * 2 * ROWS, 2 * ROWS)
        ended(tok_a.at[pl.ds(0, TOK), pair], tl_sem.at[group])
        ended(tok_a.at[pl.ds(TOK, TOK), pair], tr_sem.at[group])

    def product(q, group):
        return jnp.dot(
            cot_t[q], tok_a[:, pl.ds(group * 2 * ROWS, 2 * ROWS)], preferred_element_type=F32
        )

    def weights_y(q, first):
        for copy in send_w_y(q):
            copy.start()

    def weights_x(q, first):
        send_w_x(q, OWN).start()

    def issue_far(q, first):
        @pl.when(first)
        def _():
            loads[1].wait()
            tokens_ready(0)

        swap_cot(q).wait_recv()
        for n in range(2):
            cot_t[q, :, pl.ds(n * TOK, TOK)] = cot[n, :, quarter(q)].T
        far = product(q, 0)
        s1_out[q, 0] = far[:HALF].astype(BF16)
        s1_out[q, 1] = far[HALF:].astype(BF16)
        for copy in send_s1(q):
            copy.start()

    def issue_near(q, first):
        @pl.when(first)
        def _():
            tokens_ready(1)

        after = product(q, 1)
        d_out[q, 0] = after[HALF:].astype(BF16)
        send_d(q)[0].start()
        r_acc[q, 0] = after[:HALF]

        @pl.when(first)
        def _():
            tokens_ready(2)

        before = product(q, 2)
        d_out[q, 1] = before[:HALF].astype(BF16)
        send_d(q)[1].start()
        r_acc[q, 1] = before[HALF:]

    def issue_own(q, first):
        @pl.when(first)
        def _():
            tokens_ready(3)

        own_acc[q] = product(q, 3)

    def relay(q, first):
        ended(s1_in.at[q], s1_r.at[q])
        for n in range(2):
            r_out[q, n] = (r_acc[q, n] + s1_in[q, n].astype(F32)).astype(BF16)
            send_r(q)[n].start()

    def gather_sum(q, first):
        ended(d_in.at[q], d_r.at[q])
        ended(r_in.at[q], r_r.at[q])
        top = own_acc[q, :HALF] + r_in[q, 0].astype(F32) + d_in[q, 1].astype(F32)
        low = own_acc[q, HALF:] + d_in[q, 0].astype(F32) + r_in[q, 1].astype(F32)
        x_out[q, :HALF] = top[:, ROWS:].astype(BF16)
        x_out[q, HALF:] = low[:, ROWS:].astype(BF16)
        send_x(q).start()
        own_acc[q, :HALF, :ROWS] = top[:, :ROWS]
        own_acc[q, HALF:, :ROWS] = low[:, :ROWS]

    def update(q, first):
        @pl.when(first)
        def _():
            loads[2].wait()
            loads[3].wait()

        send_x(q).wait_recv()
        gradient = (own_acc[q, :, :ROWS] + x_in[q].astype(F32)).T
        fresh = beta_one * mom[:, quarter(q)] + (1.0 - beta_one) * gradient
        second = beta_two * sec[:, quarter(q)] + (1.0 - beta_two) * (gradient * gradient)
        go_out[q, 0] = fresh.astype(BF16)
        go_out[q, 1] = second.astype(BF16)
        (leg_states if two_legs else send_go)(q).start()
        mom[:, quarter(q)] = fresh
        sec[:, quarter(q)] = second
        par[:, quarter(q)] = adam(par[:, quarter(q)], fresh, second)

    def near_y(q, first):
        ended(weights.at[q, 0, pl.ds(NXT * ROWS, 2 * ROWS)], wy_r.at[q])
        onward = send_w_opp(q)
        for n, i in ((0, PRV), (1, NXT)):
            onward[n].start()
            send_w_core(q, i).start()

    def near_y_to_x(q, first):
        send_w_x(q, PRV).start()
        send_w_x(q, NXT).start()

    def across_own(q, first):
        send_w_x(q, OWN).wait_recv()
        send_w_core(q, OWN + 1).start()

    def across_to_y(q, first):
        for copy in send_w_z(q):
            copy.start()

    def far_y(q, first):
        ended(w(q, OPP), wo_r.at[q])
        send_w_x(q, OPP).start()
        send_w_core(q, OPP).start()

    def across_near(q, first):
        for i in (PRV, NXT):
            send_w_x(q, i).wait_recv()
            send_w_core(q, i + 1).start()

    def across_far(q, first):
        send_w_x(q, OPP).wait_recv()
        send_w_core(q, OPP + 1).start()

    def near_z(q, first):
        ended(weights.at[q, 0, pl.ds(NXT * ROWS, 2 * ROWS)], wz_r.at[q])
        onward = send_w_far(q)
        for n, i in ((0, PRV + 1), (1, NXT + 1)):
            onward[n].start()
            send_w_core(q, i).start()

    def far_both(q, first):
        ended(w(q, OPP), wo_r.at[q])
        send_w_core(q, OPP).start()
        ended(w(q, OPP + 1), wq_r.at[q])
        send_w_core(q, OPP + 1).start()

    def activation_part(q, slots, rows):
        total = jnp.dot(tok_a[rows, slots], weights[q, 0, slots], preferred_element_type=F32)
        return total + jnp.dot(
            tok_b[rows, slots], weights[q, 1, slots], preferred_element_type=F32
        )

    def halves(body):
        @pl.loop(0, 2)
        def _(n):
            body(pl.ds(pl.multiple_of(n * (TOK // 2), TOK // 2), TOK // 2))

    last, others = pl.ds(0, 2 * ROWS), pl.ds(2 * ROWS, 6 * ROWS)

    def activation_most(q, first):
        @pl.when(first)
        def _():
            ended(tok_b, tl_sem.at[4])

        ended(weights.at[q, 1, others], wc_r.at[q, 1])

        @halves
        def _(rows):
            act_acc[q, rows] = activation_part(q, others, rows)

    def activation_rest(q, first):
        ended(weights.at[q, 1, last], wc_r.at[q, 0])

        @halves
        def _(rows):
            total = act_acc[q, rows] + activation_part(q, last, rows)
            act_v[q, rows] = total.astype(BF16)

        store_act(q).start()

    store_nw = pltpu.make_async_copy(nw_ref, nw_hbm, nw_sem.at[0])

    def store_act(q):
        return pltpu.make_async_copy(act_v.at[q], act_hbm.at[:, quarter(q)], sa_sem.at[q])

    def params_x(q, first):
        leg_params(q).start()

    def pass_on(q, first):
        leg_params(q).wait_recv()
        leg_states(q).wait_recv()
        send_go(q).start()

    def turn_back(q, first):
        leg_one.wait_recv()
        leg_two.start()

    def mix(q, first):
        @pl.when(first)
        def _():
            if not two_legs:
                send_p.wait_recv()
            if two_ways:
                leg_two.wait_recv()
            send_pw.wait_recv()
            nw_ref[0] = 0.5 * (pw_ref[0] + pw_in[0, 0])
            store_nw.start()

        send_go(q).wait_recv()
        theirs = go_in[q, 0].astype(F32)
        second = go_in[q, 1].astype(F32)
        param = go_in[q, 2] if two_legs else par_r[:, quarter(q)]
        stepped = adam(param.astype(F32), theirs, second)
        par[:, quarter(q)] = 0.5 * (par[:, quarter(q)] + stepped)
        mom[:, quarter(q)] = 0.5 * (mom[:, quarter(q)] + theirs)
        sec[:, quarter(q)] = 0.5 * (sec[:, quarter(q)] + second)

    events = {
        event.__name__: event
        for event in (
            weights_y, weights_x, issue_far, issue_near, issue_own, relay, gather_sum, update,
            near_y, near_y_to_x, across_own, across_to_y, far_y, across_near, across_far,
            near_z, far_both, activation_most, activation_rest, mix, turn_back,
            params_x, pass_on,
        )
    }
    for n in turns:
        send_w_core(n, OWN).start()

    def run(i, _):
        for name, places in order.items():
            places = {q: n for q, n in enumerate(places) if n >= 0}
            here, q = False, 0
            for turn, n in places.items():
                here = jnp.logical_or(here, i == n)
                q = q + turn * (i == n).astype(jnp.int32)
            event = events[name]

            @pl.when(here)
            def _():
                event(q, i == min(places.values()))

        return 0

    passes = 1 + max(max(places) for places in order.values())
    lax.fori_loop(0, passes, run, 0)

    def finish():
        around = sum(n >= 0 for n in order.get("across_to_y", ()))
        across = QUARTERS + 3 * (QUARTERS - around)
        ended(tok_a.at[pl.ds(TOK, TOK)], ts_sem.at[0])
        ended(cot.at[1], ts_sem.at[1])
        ended(weights.at[:, 0], wc_s.at[0])
        ended(weights.at[0, 0], wy_s.at[0])
        ended(weights.at[0, 0, pl.ds(0, 4 * ROWS)], wo_s.at[0])
        if around:
            ended(weights.at[0, 0, pl.ds(0, 2 * around * ROWS)], wz_s.at[0])
            ended(weights.at[0, 0, pl.ds(0, around * ROWS)], wq_s.at[0])
        ended(tok_b.at[pl.ds(0, across * (TOK // 16))], wx_s.at[0])
        ended(s1_out, s1_s.at[0])
        ended(d_out, d_s.at[0])
        ended(r_out, r_s.at[0])
        ended(x_out, x_s.at[0])
        if two_legs:
            ended(go_out, gl_s.at[0])
            ended(par_b, gq_s.at[0])
            ended(go_relay, go_s.at[0])
        else:
            ended(go_out, go_s.at[0])
            send_p.wait_send()
        send_pw.wait_send()
        for q in range(QUARTERS):
            store_act(q).wait()
        store_nw.wait()
        if two_ways:
            leg_one.wait_send()
            leg_two.wait_send()

    finish()


def leave_kernel(*refs):
    states, act, new_states, new_act, held, sems = refs[:3], refs[3], refs[4:7], refs[7], *refs[8:]
    blocks = [pl.ds(n * TOK // 4, TOK // 4) for n in range(4)]
    loads = [
        pltpu.make_async_copy(act.at[rows], held.at[rows], sems.at[n])
        for n, rows in enumerate(blocks)
    ]
    parts = [pl.ds(n * ROWS // 2, ROWS // 2) for n in range(2)]
    copies = [
        pltpu.make_async_copy(src.at[rows], dst.at[rows], sems.at[8 + 2 * n + k])
        for n, (src, dst) in enumerate(zip(states, new_states))
        for k, rows in enumerate(parts)
    ]
    stores = [
        pltpu.make_async_copy(held.at[rows], new_act.at[rows], sems.at[4 + n])
        for n, rows in enumerate(blocks)
    ]
    for copy in loads + copies:
        copy.start()
    for load, store in zip(loads, stores):
        load.wait()
        store.start()
    for copy in copies + stores:
        copy.wait()


def leave(states, activation):
    arrays = [pltpu.with_memory_space_constraint(a, pltpu.VMEM) for a in states] + [activation]
    return pl.pallas_call(
        leave_kernel,
        out_shape=tuple(jax.ShapeDtypeStruct(a.shape, a.dtype) for a in arrays),
        in_specs=[pl.BlockSpec(memory_space=pltpu.VMEM)] * len(states)
        + [pl.BlockSpec(memory_space=pl.ANY)],
        out_specs=tuple(pl.BlockSpec(memory_space=pl.ANY) for _ in arrays),
        scratch_shapes=[pltpu.VMEM((TOK, FF), BF16), pltpu.SemaphoreType.DMA((14,))],
        compiler_params=pltpu.CompilerParams(vmem_limit_bytes=8 << 20),
        name="leave",
    )(*arrays)


def step_kernel(offset, collective_id):
    any_spec = pl.BlockSpec(memory_space=pl.ANY)
    smem = pl.BlockSpec(memory_space=pltpu.SMEM)
    vmem = pl.BlockSpec(memory_space=pltpu.VMEM)
    Q = QUARTERS
    dma = pltpu.SemaphoreType.DMA
    scratch = [
        pltpu.VMEM((2 * TOK, 8 * ROWS), BF16),
        pltpu.VMEM((TOK, 8 * ROWS), BF16),
        pltpu.VMEM((2, TOK, FF), BF16),
        pltpu.VMEM((Q, QC, 2 * TOK), BF16),
        pltpu.VMEM((ROWS, FF), BF16),
        pltpu.VMEM((ROWS, FF), BF16),
        pltpu.VMEM((ROWS // 2, FF), BF16),
        pltpu.VMEM((Q, 2, 8 * ROWS, QC), BF16),
    ]
    scratch += [pltpu.VMEM((Q, 2, HALF, 2 * ROWS), BF16)] * 6
    scratch += [
        pltpu.VMEM((Q, 2, HALF, 2 * ROWS), F32),
        pltpu.VMEM((Q, QC, 2 * ROWS), F32),
        pltpu.VMEM((Q, QC, ROWS), BF16),
        pltpu.VMEM((Q, QC, ROWS), BF16),
        pltpu.VMEM((Q, 2, ROWS, QC), BF16),
        pltpu.VMEM((Q, 3 if offset == 1 else 2, ROWS, QC), BF16),
        pltpu.VMEM((Q, 3, ROWS, QC) if offset == 1 else (16, 128), BF16),
        pltpu.VMEM((8, 128), F32),
        pltpu.VMEM((8, 128), F32),
        pltpu.SMEM((1,), F32),
        pltpu.VMEM((Q, TOK, QC), F32),
        pltpu.VMEM((Q, TOK, QC), BF16),
        dma((4,)), dma((5,)), dma((2,)), dma((4,)), dma((Q,)),
        dma((1,)), dma((Q,)), dma((1,)), dma((Q,)),
        dma((1,)), dma((Q,)), dma((1,)), dma((Q,)),
        dma((1,)), dma((Q, 4)), dma((1,)), dma((Q, 2)),
        dma((1,)), dma((Q,)), dma((1,)), dma((Q,)), dma((1,)), dma((Q,)),
        dma((1,)), dma((Q,)),
        dma((6,)), dma((2,)), dma((1,)), dma((Q,)), dma((1,)), dma((Q,)), dma((1,)), dma((Q,)),
        dma((Q,)), dma((1,)),
    ]
    return pl.pallas_call(
        functools.partial(kernel, offset, ORDERS[offset]),
        out_shape=(
            pltpu.VMEM((ROWS, FF), F32),
            pltpu.VMEM((ROWS, FF), F32),
            pltpu.VMEM((ROWS, FF), F32),
            jax.ShapeDtypeStruct((1,), F32),
            jax.ShapeDtypeStruct((TOK, FF), BF16),
        ),
        in_specs=[any_spec, any_spec, any_spec, smem, any_spec, any_spec],
        out_specs=(vmem, vmem, vmem, any_spec, any_spec),
        scratch_shapes=scratch,
        compiler_params=pltpu.CompilerParams(
            collective_id=collective_id, has_side_effects=True, vmem_limit_bytes=48 << 20
        ),
        name=f"push_step_{offset}",
    )


def per_device(params, first_moment, second_moment, push_weight, tokens, cotangent, gossip_round):
    levels = REPLICAS.bit_length() - 1
    branches = [step_kernel(1 << level, level + 1) for level in range(levels)]
    new_params, new_first, new_second, new_weight, activation = lax.switch(
        gossip_round[0] % levels,
        branches,
        params[0], first_moment[0], second_moment[0], push_weight, tokens[0], cotangent[0],
    )
    new_params, new_first, new_second, activation = leave(
        (new_params, new_first, new_second), activation
    )
    return (new_params[None], new_first[None], new_second[None], new_weight, activation[None])


def solution(mesh):
    rows = P("replica", "shard", None)
    return jax.shard_map(
        per_device,
        mesh=mesh,
        in_specs=(rows, rows, rows, P("replica"), rows, rows, P()),
        out_specs=(rows, rows, rows, P("replica"), rows),
        check_vma=False,
    )
```

```python
import functools

import jax
import jax.numpy as jnp
from jax import lax
from jax.experimental import pallas as pl
from jax.experimental.pallas import tpu as pltpu
from jax.sharding import PartitionSpec as P

STEP_COUNT = 20

beta_one = 0.9
beta_two = 0.999
rate = 0.003
epsilon = 1e-08

MESH = pl.DeviceIdType.MESH
REPLICAS = 16
ROWS = 256
FF = 1024
TOK = 512
QUARTERS = 4
QC = FF // QUARTERS
HALF = QC // 2
F32 = jnp.float32
BF16 = jnp.bfloat16

OPP, NXT, PRV, OWN = 0, 2, 4, 6


ORDERS = {
    1: dict(
        across_far=(24, -1, -1, -1),
        across_own=(21, 3, 7, 12),
        weights_y=(2, 13, 12, 20),
        gather_sum=(15, 8, 10, 14),
        issue_far=(8, 2, 4, 7),
        params_x=(5, 3, 9, 6),
        weights_x=(20, 1, 0, 2),
        near_y_to_x=(20, -1, -1, -1),
        across_to_y=(-1, 15, 13, 16),
        update=(17, 10, 11, 16),
        near_z=(-1, 19, 20, 21),
        activation_most=(24, 20, 22, 23),
        across_near=(23, -1, -1, -1),
        activation_rest=(25, 21, 23, 24),
        far_y=(20, -1, -1, -1),
        pass_on=(20, 13, 14, 18),
        issue_near=(11, 2, 5, 10),
        relay=(11, 4, 6, 10),
        issue_own=(8, 3, 6, 9),
        mix=(25, 17, 18, 21),
        near_y=(11, 19, 20, 21),
        far_both=(-1, 20, 22, 23),
    ),
    2: dict(
        activation_most=(11, 20, 13, 21),
        across_near=(10, 19, 9, -1),
        far_y=(5, 19, 10, -1),
        near_z=(-1, -1, -1, 20),
        relay=(10, 15, 4, 12),
        near_y=(3, 16, 4, 19),
        near_y_to_x=(3, 16, 4, -1),
        issue_far=(5, 13, 3, 7),
        across_far=(10, 20, 13, -1),
        gather_sum=(13, 17, 8, 14),
        weights_x=(1, 10, 2, 14),
        issue_near=(9, 14, 3, 10),
        activation_rest=(12, 20, 13, 21),
        issue_own=(8, 13, 3, 7),
        update=(13, 19, 11, 15),
        weights_y=(0, 13, 2, 16),
        mix=(18, 21, 13, 17),
        far_both=(-1, -1, -1, 20),
        across_own=(5, 15, 6, 18),
        across_to_y=(-1, -1, -1, 18),
    ),
    4: dict(
        issue_near=(6, 2, 10, 5),
        issue_own=(6, 2, 9, 4),
        weights_x=(1, 0, 2, 3),
        relay=(7, 2, 10, 5),
        far_both=(-1, -1, -1, 17),
        weights_y=(12, 0, 9, 11),
        across_to_y=(-1, -1, -1, 14),
        across_near=(17, 7, 16, -1),
        far_y=(16, 7, 15, -1),
        near_y=(15, 3, 10, 14),
        issue_far=(5, 1, 8, 2),
        near_y_to_x=(15, 5, 10, -1),
        update=(11, 5, 14, 7),
        across_far=(19, 9, 16, -1),
        activation_most=(19, 8, 17, 16),
        across_own=(12, 2, 10, 6),
        near_z=(-1, -1, -1, 15),
        turn_back=(5, -1, -1, -1),
        gather_sum=(9, 3, 13, 6),
        activation_rest=(19, 9, 17, 18),
        mix=(15, 12, 19, 13),
    ),
    8: dict(
        across_own=(12, 4, 9, 15),
        weights_y=(11, 0, 1, 15),
        across_to_y=(-1, -1, -1, 15),
        far_y=(16, 4, 11, -1),
        activation_rest=(18, 6, 15, 19),
        issue_own=(11, 5, 4, 9),
        weights_x=(1, 3, 2, 7),
        update=(17, 10, 6, 13),
        issue_far=(9, 4, 3, 6),
        gather_sum=(15, 7, 4, 10),
        across_far=(17, 5, 14, -1),
        near_z=(-1, -1, -1, 17),
        near_y=(14, 2, 8, 17),
        activation_most=(16, 5, 13, 18),
        across_near=(15, 4, 12, -1),
        near_y_to_x=(14, 3, 8, -1),
        issue_near=(12, 4, 3, 7),
        relay=(13, 5, 3, 7),
        far_both=(-1, -1, -1, 18),
        mix=(19, 15, 12, 18),
    ),
}


def adam(param, first, second):
    correct_one = 1.0 - beta_one ** (STEP_COUNT + 1)
    correct_two = 1.0 - beta_two ** (STEP_COUNT + 1)
    scaled = first * (rate / correct_one)
    return param - scaled / (jnp.sqrt(second * (1.0 / correct_two)) + epsilon)


def kernel(
    offset, order,
    p_hbm, m_hbm, v_hbm, pw_ref, tok_hbm, cot_hbm,
    par, mom, sec, nw_hbm, act_hbm,
    tok_a, tok_b, cot, cot_t, par_b, par_r, par_relay, weights,
    s1_out, s1_in, d_out, d_in, r_out, r_in, r_acc, own_acc, x_out, x_in,
    go_out, go_in, go_relay, pw_out, pw_in, nw_ref, act_acc, act_v,
    load_sem, tl_sem, ts_sem, tr_sem, cs_sem,
    wy_s, wy_r, wo_s, wo_r, wz_s, wz_r, wq_s, wq_r, wx_s, wx_r, wc_s, wc_r,
    s1_s, s1_r, d_s, d_r, r_s, r_r, x_s, x_r,
    gp_sem, gw_sem, go_s, go_r, gl_s, gl_r, gq_s, gq_r, sa_sem, nw_sem,
):
    r = lax.axis_index("replica")
    s = lax.axis_index("shard")
    c = lax.rem(s, 2)
    x = lax.rem(lax.div(s, 2), 2)
    y = lax.div(s, 4)
    ys = [lax.rem(y + 2, 4), lax.rem(y + 1, 4), lax.rem(y + 3, 4), y]

    def at(yy, xx, cc):
        return (r, (yy * 2 + xx) * 2 + cc)

    up, down = at(ys[1], x, c), at(ys[2], x, c)
    across, sibling = at(y, 1 - x, c), at(y, x, 1 - c)
    two_legs = offset == 1
    peer = s if not two_legs else at(y, 1 - x, c)[1]
    ahead = (lax.rem(r + offset, REPLICAS), peer)
    behind = (lax.rem(r + REPLICAS - offset, REPLICAS), peer)

    def remote(src, dst, ss, rs, to):
        return pltpu.make_async_remote_copy(
            src_ref=src, dst_ref=dst, send_sem=ss, recv_sem=rs, device_id=to, device_id_type=MESH
        )

    def columns(i, core):
        block = ys[i // 2] * 2 + (x if i % 2 == 0 else 1 - x)
        return pl.ds(pl.multiple_of((block * 2 + core) * ROWS, ROWS), ROWS)

    def place(i):
        return pl.ds(i * ROWS, ROWS)

    loads = [
        pltpu.make_async_copy(p_hbm, par, load_sem.at[0]),
        pltpu.make_async_copy(cot_hbm, cot.at[0], load_sem.at[1]),
        pltpu.make_async_copy(m_hbm, mom, load_sem.at[2]),
        pltpu.make_async_copy(v_hbm, sec, load_sem.at[3]),
    ]
    load_a = [
        pltpu.make_async_copy(
            tok_hbm.at[:, columns(i, c)], tok_a.at[pl.ds(0, TOK), place(i)], tl_sem.at[i // 2]
        )
        for i in range(8)
    ]
    load_b = [
        pltpu.make_async_copy(
            tok_hbm.at[:, columns(i, 1 - c)], tok_b.at[:, place(i)], tl_sem.at[4]
        )
        for i in range(8)
    ]
    loads[0].start()
    loads[1].start()
    for copy in load_a:
        copy.start()

    barrier = pltpu.get_barrier_semaphore()
    partners = [up, down, across, sibling, ahead, behind]
    back = (lax.rem(r + REPLICAS - 6, REPLICAS), s)
    if offset == 4:
        partners += [back, (lax.rem(r + 6, REPLICAS), s)]
    for to in partners:
        pl.semaphore_signal(barrier, inc=1, device_id=to, device_id_type=MESH)
    pl.semaphore_wait(barrier, len(partners))

    def quarter(q):
        return pl.ds(pl.multiple_of(q * QC, QC), QC)

    def swap_cot(q):
        return remote(
            cot_hbm.at[:, quarter(q)], cot.at[1, :, quarter(q)],
            ts_sem.at[1], cs_sem.at[q], sibling,
        )

    swap_tok = [
        remote(
            tok_hbm.at[:, columns(i, 1 - c)],
            tok_a.at[pl.ds(TOK, TOK), place(i)],
            ts_sem.at[0], tr_sem.at[i // 2], sibling,
        )
        for i in range(8)
    ]
    turns = sorted(range(QUARTERS), key=lambda q: order["issue_far"][q])
    swap_cot(turns[0]).start()
    for copy in swap_tok:
        copy.start()
    for q in turns[1:]:
        swap_cot(q).start()

    def w(q, i, parity=0):
        return weights.at[q, parity, place(i), :]

    def w_half(q, i, h):
        return weights.at[q, 0, pl.ds(i * ROWS + h * HALF, HALF), :]

    def send_w_y(q):
        return [
            remote(w(q, OWN), w(q, PRV), wy_s.at[0], wy_r.at[q], up),
            remote(w(q, OWN), w(q, NXT), wy_s.at[0], wy_r.at[q], down),
        ]

    def send_w_opp(q):
        return [
            remote(w_half(q, PRV, 0), w_half(q, OPP, 0), wo_s.at[0], wo_r.at[q], up),
            remote(w_half(q, NXT, 1), w_half(q, OPP, 1), wo_s.at[0], wo_r.at[q], down),
        ]

    def send_w_z(q):
        return [
            remote(w(q, OWN + 1), w(q, PRV + 1), wz_s.at[0], wz_r.at[q], up),
            remote(w(q, OWN + 1), w(q, NXT + 1), wz_s.at[0], wz_r.at[q], down),
        ]

    def send_w_far(q):
        return [
            remote(
                w_half(q, PRV + 1, 0), w_half(q, OPP + 1, 0), wq_s.at[0], wq_r.at[q], up
            ),
            remote(
                w_half(q, NXT + 1, 1), w_half(q, OPP + 1, 1), wq_s.at[0], wq_r.at[q], down
            ),
        ]

    def send_w_x(q, i):
        g = i // 2
        return remote(w(q, i), w(q, i + 1), wx_s.at[0], wx_r.at[q, g], across)

    def send_w_core(q, i):
        return remote(w(q, i), w(q, i, 1), wc_s.at[0], wc_r.at[q, min(i // 2, 1)], sibling)

    def send_s1(q):
        return [
            remote(s1_out.at[q, h], s1_in.at[q, h], s1_s.at[0], s1_r.at[q], to)
            for h, to in enumerate((up, down))
        ]

    def send_d(q):
        return [
            remote(d_out.at[q, h], d_in.at[q, h], d_s.at[0], d_r.at[q], to)
            for h, to in enumerate((up, down))
        ]

    def send_r(q):
        return [
            remote(r_out.at[q, h], r_in.at[q, h], r_s.at[0], r_r.at[q], to)
            for h, to in enumerate((up, down))
        ]

    def send_x(q):
        return remote(x_out.at[q], x_in.at[q], x_s.at[0], x_r.at[q], across)

    two_ways = offset == 4
    near_half, far_half = pl.ds(0, ROWS // 2), pl.ds(ROWS // 2, ROWS // 2)
    if two_ways:
        send_p = remote(
            par_b.at[near_half], par_r.at[near_half], gp_sem.at[0], gp_sem.at[1], ahead
        )
        leg_one = remote(par_b.at[far_half], par_relay, gp_sem.at[2], gp_sem.at[3], back)
        leg_two = remote(par_relay, par_r.at[far_half], gp_sem.at[4], gp_sem.at[5], back)
    else:
        send_p = remote(par_b, par_r, gp_sem.at[0], gp_sem.at[1], ahead)
    send_pw = remote(pw_out, pw_in, gw_sem.at[0], gw_sem.at[1], ahead)

    def send_go(q):
        source = go_relay if two_legs else go_out
        return remote(source.at[q], go_in.at[q], go_s.at[0], go_r.at[q], ahead)

    states = pl.ds(0, 2)

    def leg_states(q):
        return remote(
            go_out.at[q], go_relay.at[q, states], gl_s.at[0], gl_r.at[q], across
        )

    def leg_params(q):
        return remote(
            par_b.at[:, quarter(q)], go_relay.at[q, 2], gq_s.at[0], gq_r.at[q], across
        )

    loads[0].wait()
    par_b[...] = par[...].astype(BF16)
    if two_ways:
        leg_one.start()
    if not two_legs:
        send_p.start()
    pw_out[...] = jnp.full(pw_out.shape, pw_ref[0], F32)
    send_pw.start()

    @pl.loop(0, QUARTERS)
    def _(q):
        weights[q, 0, place(OWN), :] = (par[:, quarter(q)] / pw_ref[0]).astype(BF16)

    loads[2].start()
    loads[3].start()
    for copy in load_b:
        copy.start()

    def ended(ref, sem):
        pltpu.make_async_copy(ref, ref, sem).wait()

    def tokens_ready(group):
        pair = pl.ds(group * 2 * ROWS, 2 * ROWS)
        ended(tok_a.at[pl.ds(0, TOK), pair], tl_sem.at[group])
        ended(tok_a.at[pl.ds(TOK, TOK), pair], tr_sem.at[group])

    def product(q, group):
        return jnp.dot(
            cot_t[q], tok_a[:, pl.ds(group * 2 * ROWS, 2 * ROWS)], preferred_element_type=F32
        )

    def weights_y(q, first):
        for copy in send_w_y(q):
            copy.start()

    def weights_x(q, first):
        send_w_x(q, OWN).start()

    def issue_far(q, first):
        @pl.when(first)
        def _():
            loads[1].wait()
            tokens_ready(0)

        swap_cot(q).wait_recv()
        for n in range(2):
            cot_t[q, :, pl.ds(n * TOK, TOK)] = cot[n, :, quarter(q)].T
        far = product(q, 0)
        s1_out[q, 0] = far[:HALF].astype(BF16)
        s1_out[q, 1] = far[HALF:].astype(BF16)
        for copy in send_s1(q):
            copy.start()

    def issue_near(q, first):
        @pl.when(first)
        def _():
            tokens_ready(1)

        after = product(q, 1)
        d_out[q, 0] = after[HALF:].astype(BF16)
        send_d(q)[0].start()
        r_acc[q, 0] = after[:HALF]

        @pl.when(first)
        def _():
            tokens_ready(2)

        before = product(q, 2)
        d_out[q, 1] = before[:HALF].astype(BF16)
        send_d(q)[1].start()
        r_acc[q, 1] = before[HALF:]

    def issue_own(q, first):
        @pl.when(first)
        def _():
            tokens_ready(3)

        own_acc[q] = product(q, 3)

    def relay(q, first):
        ended(s1_in.at[q], s1_r.at[q])
        for n in range(2):
            r_out[q, n] = (r_acc[q, n] + s1_in[q, n].astype(F32)).astype(BF16)
            send_r(q)[n].start()

    def gather_sum(q, first):
        ended(d_in.at[q], d_r.at[q])
        ended(r_in.at[q], r_r.at[q])
        top = own_acc[q, :HALF] + r_in[q, 0].astype(F32) + d_in[q, 1].astype(F32)
        low = own_acc[q, HALF:] + d_in[q, 0].astype(F32) + r_in[q, 1].astype(F32)
        x_out[q, :HALF] = top[:, ROWS:].astype(BF16)
        x_out[q, HALF:] = low[:, ROWS:].astype(BF16)
        send_x(q).start()
        own_acc[q, :HALF, :ROWS] = top[:, :ROWS]
        own_acc[q, HALF:, :ROWS] = low[:, :ROWS]

    def update(q, first):
        @pl.when(first)
        def _():
            loads[2].wait()
            loads[3].wait()

        send_x(q).wait_recv()
        gradient = (own_acc[q, :, :ROWS] + x_in[q].astype(F32)).T
        fresh = beta_one * mom[:, quarter(q)] + (1.0 - beta_one) * gradient
        second = beta_two * sec[:, quarter(q)] + (1.0 - beta_two) * (gradient * gradient)
        go_out[q, 0] = fresh.astype(BF16)
        go_out[q, 1] = second.astype(BF16)
        (leg_states if two_legs else send_go)(q).start()
        mom[:, quarter(q)] = fresh
        sec[:, quarter(q)] = second
        par[:, quarter(q)] = adam(par[:, quarter(q)], fresh, second)

    def near_y(q, first):
        ended(weights.at[q, 0, pl.ds(NXT * ROWS, 2 * ROWS)], wy_r.at[q])
        onward = send_w_opp(q)
        for n, i in ((0, PRV), (1, NXT)):
            onward[n].start()
            send_w_core(q, i).start()

    def near_y_to_x(q, first):
        send_w_x(q, PRV).start()
        send_w_x(q, NXT).start()

    def across_own(q, first):
        send_w_x(q, OWN).wait_recv()
        send_w_core(q, OWN + 1).start()

    def across_to_y(q, first):
        for copy in send_w_z(q):
            copy.start()

    def far_y(q, first):
        ended(w(q, OPP), wo_r.at[q])
        send_w_x(q, OPP).start()
        send_w_core(q, OPP).start()

    def across_near(q, first):
        for i in (PRV, NXT):
            send_w_x(q, i).wait_recv()
            send_w_core(q, i + 1).start()

    def across_far(q, first):
        send_w_x(q, OPP).wait_recv()
        send_w_core(q, OPP + 1).start()

    def near_z(q, first):
        ended(weights.at[q, 0, pl.ds(NXT * ROWS, 2 * ROWS)], wz_r.at[q])
        onward = send_w_far(q)
        for n, i in ((0, PRV + 1), (1, NXT + 1)):
            onward[n].start()
            send_w_core(q, i).start()

    def far_both(q, first):
        ended(w(q, OPP), wo_r.at[q])
        send_w_core(q, OPP).start()
        ended(w(q, OPP + 1), wq_r.at[q])
        send_w_core(q, OPP + 1).start()

    def activation_part(q, slots, rows):
        total = jnp.dot(tok_a[rows, slots], weights[q, 0, slots], preferred_element_type=F32)
        return total + jnp.dot(
            tok_b[rows, slots], weights[q, 1, slots], preferred_element_type=F32
        )

    def halves(body):
        @pl.loop(0, 2)
        def _(n):
            body(pl.ds(pl.multiple_of(n * (TOK // 2), TOK // 2), TOK // 2))

    last, others = pl.ds(0, 2 * ROWS), pl.ds(2 * ROWS, 6 * ROWS)

    def activation_most(q, first):
        @pl.when(first)
        def _():
            ended(tok_b, tl_sem.at[4])

        ended(weights.at[q, 1, others], wc_r.at[q, 1])

        @halves
        def _(rows):
            act_acc[q, rows] = activation_part(q, others, rows)

    def activation_rest(q, first):
        ended(weights.at[q, 1, last], wc_r.at[q, 0])

        @halves
        def _(rows):
            total = act_acc[q, rows] + activation_part(q, last, rows)
            act_v[q, rows] = total.astype(BF16)

        store_act(q).start()

    store_nw = pltpu.make_async_copy(nw_ref, nw_hbm, nw_sem.at[0])

    def store_act(q):
        return pltpu.make_async_copy(act_v.at[q], act_hbm.at[:, quarter(q)], sa_sem.at[q])

    def params_x(q, first):
        leg_params(q).start()

    def pass_on(q, first):
        leg_params(q).wait_recv()
        leg_states(q).wait_recv()
        send_go(q).start()

    def turn_back(q, first):
        leg_one.wait_recv()
        leg_two.start()

    def mix(q, first):
        @pl.when(first)
        def _():
            if not two_legs:
                send_p.wait_recv()
            if two_ways:
                leg_two.wait_recv()
            send_pw.wait_recv()
            nw_ref[0] = 0.5 * (pw_ref[0] + pw_in[0, 0])
            store_nw.start()

        send_go(q).wait_recv()
        theirs = go_in[q, 0].astype(F32)
        second = go_in[q, 1].astype(F32)
        param = go_in[q, 2] if two_legs else par_r[:, quarter(q)]
        stepped = adam(param.astype(F32), theirs, second)
        par[:, quarter(q)] = 0.5 * (par[:, quarter(q)] + stepped)
        mom[:, quarter(q)] = 0.5 * (mom[:, quarter(q)] + theirs)
        sec[:, quarter(q)] = 0.5 * (sec[:, quarter(q)] + second)

    events = {
        event.__name__: event
        for event in (
            weights_y, weights_x, issue_far, issue_near, issue_own, relay, gather_sum, update,
            near_y, near_y_to_x, across_own, across_to_y, far_y, across_near, across_far,
            near_z, far_both, activation_most, activation_rest, mix, turn_back,
            params_x, pass_on,
        )
    }
    for n in turns:
        send_w_core(n, OWN).start()

    def run(i, _):
        for name, places in order.items():
            places = {q: n for q, n in enumerate(places) if n >= 0}
            here = functools.reduce(jnp.logical_or, [i == n for n in places.values()])
            event = events[name]

            @pl.when(here)
            def _():
                turns_here = [turn * (i == n).astype(jnp.int32) for turn, n in places.items()]
                event(functools.reduce(jnp.add, turns_here), i == min(places.values()))

        return 0

    passes = 1 + max(max(places) for places in order.values())
    lax.fori_loop(0, passes, run, 0)

    def finish():
        around = sum(n >= 0 for n in order.get("across_to_y", ()))
        across = QUARTERS + 3 * (QUARTERS - around)
        ended(tok_a.at[pl.ds(TOK, TOK)], ts_sem.at[0])
        ended(cot.at[1], ts_sem.at[1])
        ended(weights.at[:, 0], wc_s.at[0])
        ended(weights.at[0, 0], wy_s.at[0])
        ended(weights.at[0, 0, pl.ds(0, 4 * ROWS)], wo_s.at[0])
        if around:
            ended(weights.at[0, 0, pl.ds(0, 2 * around * ROWS)], wz_s.at[0])
            ended(weights.at[0, 0, pl.ds(0, around * ROWS)], wq_s.at[0])
        ended(tok_b.at[pl.ds(0, across * (TOK // 16))], wx_s.at[0])
        ended(s1_out, s1_s.at[0])
        ended(d_out, d_s.at[0])
        ended(r_out, r_s.at[0])
        ended(x_out, x_s.at[0])
        if two_legs:
            ended(go_out, gl_s.at[0])
            ended(par_b, gq_s.at[0])
            ended(go_relay, go_s.at[0])
        else:
            ended(go_out, go_s.at[0])
            send_p.wait_send()
        send_pw.wait_send()
        for q in range(QUARTERS):
            store_act(q).wait()
        store_nw.wait()
        if two_ways:
            leg_one.wait_send()
            leg_two.wait_send()

    finish()


def leave_kernel(*refs):
    states, act, new_states, new_act, held, sems = refs[:3], refs[3], refs[4:7], refs[7], *refs[8:]
    blocks = [pl.ds(n * TOK // 4, TOK // 4) for n in range(4)]
    loads = [
        pltpu.make_async_copy(act.at[rows], held.at[rows], sems.at[n])
        for n, rows in enumerate(blocks)
    ]
    parts = [pl.ds(n * ROWS // 2, ROWS // 2) for n in range(2)]
    copies = [
        pltpu.make_async_copy(src.at[rows], dst.at[rows], sems.at[8 + 2 * n + k])
        for n, (src, dst) in enumerate(zip(states, new_states))
        for k, rows in enumerate(parts)
    ]
    stores = [
        pltpu.make_async_copy(held.at[rows], new_act.at[rows], sems.at[4 + n])
        for n, rows in enumerate(blocks)
    ]
    for copy in loads + copies:
        copy.start()
    for load, store in zip(loads, stores):
        load.wait()
        store.start()
    for copy in copies + stores:
        copy.wait()


def leave(states, activation):
    arrays = [pltpu.with_memory_space_constraint(a, pltpu.VMEM) for a in states] + [activation]
    return pl.pallas_call(
        leave_kernel,
        out_shape=tuple(jax.ShapeDtypeStruct(a.shape, a.dtype) for a in arrays),
        in_specs=[pl.BlockSpec(memory_space=pltpu.VMEM)] * len(states)
        + [pl.BlockSpec(memory_space=pl.ANY)],
        out_specs=tuple(pl.BlockSpec(memory_space=pl.ANY) for _ in arrays),
        scratch_shapes=[pltpu.VMEM((TOK, FF), BF16), pltpu.SemaphoreType.DMA((14,))],
        compiler_params=pltpu.CompilerParams(vmem_limit_bytes=8 << 20),
        name="leave",
    )(*arrays)


def step_kernel(offset, collective_id):
    any_spec = pl.BlockSpec(memory_space=pl.ANY)
    smem = pl.BlockSpec(memory_space=pltpu.SMEM)
    vmem = pl.BlockSpec(memory_space=pltpu.VMEM)
    Q = QUARTERS
    dma = pltpu.SemaphoreType.DMA
    scratch = [
        pltpu.VMEM((2 * TOK, 8 * ROWS), BF16),
        pltpu.VMEM((TOK, 8 * ROWS), BF16),
        pltpu.VMEM((2, TOK, FF), BF16),
        pltpu.VMEM((Q, QC, 2 * TOK), BF16),
        pltpu.VMEM((ROWS, FF), BF16),
        pltpu.VMEM((ROWS, FF), BF16),
        pltpu.VMEM((ROWS // 2, FF), BF16),
        pltpu.VMEM((Q, 2, 8 * ROWS, QC), BF16),
    ]
    scratch += [pltpu.VMEM((Q, 2, HALF, 2 * ROWS), BF16)] * 6
    scratch += [
        pltpu.VMEM((Q, 2, HALF, 2 * ROWS), F32),
        pltpu.VMEM((Q, QC, 2 * ROWS), F32),
        pltpu.VMEM((Q, QC, ROWS), BF16),
        pltpu.VMEM((Q, QC, ROWS), BF16),
        pltpu.VMEM((Q, 2, ROWS, QC), BF16),
        pltpu.VMEM((Q, 3 if offset == 1 else 2, ROWS, QC), BF16),
        pltpu.VMEM((Q, 3, ROWS, QC) if offset == 1 else (16, 128), BF16),
        pltpu.VMEM((8, 128), F32),
        pltpu.VMEM((8, 128), F32),
        pltpu.SMEM((1,), F32),
        pltpu.VMEM((Q, TOK, QC), F32),
        pltpu.VMEM((Q, TOK, QC), BF16),
        dma((4,)), dma((5,)), dma((2,)), dma((4,)), dma((Q,)),
        dma((1,)), dma((Q,)), dma((1,)), dma((Q,)),
        dma((1,)), dma((Q,)), dma((1,)), dma((Q,)),
        dma((1,)), dma((Q, 4)), dma((1,)), dma((Q, 2)),
        dma((1,)), dma((Q,)), dma((1,)), dma((Q,)), dma((1,)), dma((Q,)),
        dma((1,)), dma((Q,)),
        dma((6,)), dma((2,)), dma((1,)), dma((Q,)), dma((1,)), dma((Q,)), dma((1,)), dma((Q,)),
        dma((Q,)), dma((1,)),
    ]
    return pl.pallas_call(
        functools.partial(kernel, offset, ORDERS[offset]),
        out_shape=(
            pltpu.VMEM((ROWS, FF), F32),
            pltpu.VMEM((ROWS, FF), F32),
            pltpu.VMEM((ROWS, FF), F32),
            jax.ShapeDtypeStruct((1,), F32),
            jax.ShapeDtypeStruct((TOK, FF), BF16),
        ),
        in_specs=[any_spec, any_spec, any_spec, smem, any_spec, any_spec],
        out_specs=(vmem, vmem, vmem, any_spec, any_spec),
        scratch_shapes=scratch,
        compiler_params=pltpu.CompilerParams(
            collective_id=collective_id, has_side_effects=True, vmem_limit_bytes=48 << 20
        ),
        name=f"push_step_{offset}",
    )


def per_device(params, first_moment, second_moment, push_weight, tokens, cotangent, gossip_round):
    levels = REPLICAS.bit_length() - 1
    branches = [step_kernel(1 << level, level + 1) for level in range(levels)]
    new_params, new_first, new_second, new_weight, activation = lax.switch(
        gossip_round[0] & (levels - 1),
        branches,
        params[0], first_moment[0], second_moment[0], push_weight, tokens[0], cotangent[0],
    )
    new_params, new_first, new_second, activation = leave(
        (new_params, new_first, new_second), activation
    )
    return (new_params[None], new_first[None], new_second[None], new_weight, activation[None])


def solution(mesh):
    rows = P("replica", "shard", None)
    return jax.shard_map(
        per_device,
        mesh=mesh,
        in_specs=(rows, rows, rows, P("replica"), rows, rows, P()),
        out_specs=(rows, rows, rows, P("replica"), rows),
        check_vma=False,
    )
```

```python
import functools

import jax
import jax.numpy as jnp
from jax import lax
from jax.experimental import pallas as pl
from jax.experimental.pallas import tpu as pltpu
from jax.sharding import PartitionSpec as P

STEP_COUNT = 20

beta_one = 0.9
beta_two = 0.999
rate = 0.003
epsilon = 1e-08

MESH = pl.DeviceIdType.MESH
REPLICAS = 16
ROWS = 256
FF = 1024
TOK = 512
QUARTERS = 4
QC = FF // QUARTERS
HALF = QC // 2
F32 = jnp.float32
BF16 = jnp.bfloat16

OPP, NXT, PRV, OWN = 0, 2, 4, 6


ORDERS = {
    1: dict(
        across_far=(-1, -1, -1, 24),
        across_own=(12, 3, 7, 21),
        weights_y=(20, 13, 12, 2),
        gather_sum=(14, 8, 10, 15),
        issue_far=(7, 2, 4, 8),
        params_x=(6, 3, 9, 5),
        weights_x=(2, 1, 0, 20),
        near_y_to_x=(-1, -1, -1, 20),
        across_to_y=(16, 15, 13, -1),
        update=(16, 10, 11, 17),
        near_z=(21, 19, 20, -1),
        activation_most=(23, 20, 22, 24),
        across_near=(-1, -1, -1, 23),
        activation_rest=(24, 21, 23, 25),
        far_y=(-1, -1, -1, 20),
        pass_on=(18, 13, 14, 20),
        issue_near=(10, 2, 5, 11),
        relay=(10, 4, 6, 11),
        issue_own=(9, 3, 6, 8),
        mix=(21, 17, 18, 25),
        near_y=(21, 19, 20, 11),
        far_both=(23, 20, 22, -1),
    ),
    2: dict(
        activation_most=(11, 20, 13, 21),
        across_near=(10, 19, 9, -1),
        far_y=(5, 19, 10, -1),
        near_z=(-1, -1, -1, 20),
        relay=(10, 15, 4, 12),
        near_y=(3, 16, 4, 19),
        near_y_to_x=(3, 16, 4, -1),
        issue_far=(5, 13, 3, 7),
        across_far=(10, 20, 13, -1),
        gather_sum=(13, 17, 8, 14),
        weights_x=(1, 10, 2, 14),
        issue_near=(9, 14, 3, 10),
        activation_rest=(12, 20, 13, 21),
        issue_own=(8, 13, 3, 7),
        update=(13, 19, 11, 15),
        weights_y=(0, 13, 2, 16),
        mix=(18, 21, 13, 17),
        far_both=(-1, -1, -1, 20),
        across_own=(5, 15, 6, 18),
        across_to_y=(-1, -1, -1, 18),
    ),
    4: dict(
        issue_near=(5, 2, 10, 6),
        issue_own=(4, 2, 9, 6),
        weights_x=(3, 0, 2, 1),
        relay=(5, 2, 10, 7),
        far_both=(17, -1, -1, -1),
        weights_y=(11, 0, 9, 12),
        across_to_y=(14, -1, -1, -1),
        across_near=(-1, 7, 16, 17),
        far_y=(-1, 7, 15, 16),
        near_y=(14, 3, 10, 15),
        issue_far=(2, 1, 8, 5),
        near_y_to_x=(-1, 5, 10, 15),
        update=(7, 5, 14, 11),
        across_far=(-1, 9, 16, 19),
        activation_most=(16, 8, 17, 19),
        across_own=(6, 2, 10, 12),
        near_z=(15, -1, -1, -1),
        turn_back=(5, -1, -1, -1),
        gather_sum=(6, 3, 13, 9),
        activation_rest=(18, 9, 17, 19),
        mix=(13, 12, 19, 15),
    ),
    8: dict(
        across_own=(12, 4, 9, 15),
        weights_y=(11, 0, 1, 15),
        across_to_y=(-1, -1, -1, 15),
        far_y=(16, 4, 11, -1),
        activation_rest=(18, 6, 15, 19),
        issue_own=(11, 5, 4, 9),
        weights_x=(1, 3, 2, 7),
        update=(17, 10, 6, 13),
        issue_far=(9, 4, 3, 6),
        gather_sum=(15, 7, 4, 10),
        across_far=(17, 5, 14, -1),
        near_z=(-1, -1, -1, 17),
        near_y=(14, 2, 8, 17),
        activation_most=(16, 5, 13, 18),
        across_near=(15, 4, 12, -1),
        near_y_to_x=(14, 3, 8, -1),
        issue_near=(12, 4, 3, 7),
        relay=(13, 5, 3, 7),
        far_both=(-1, -1, -1, 18),
        mix=(19, 15, 12, 18),
    ),
}


def adam(param, first, second):
    correct_one = 1.0 - beta_one ** (STEP_COUNT + 1)
    correct_two = 1.0 - beta_two ** (STEP_COUNT + 1)
    scaled = first * (rate / correct_one)
    return param - scaled / (jnp.sqrt(second * (1.0 / correct_two)) + epsilon)


def kernel(
    offset, order,
    p_hbm, m_hbm, v_hbm, pw_ref, tok_hbm, cot_hbm,
    par, mom, sec, nw_hbm, act_hbm, act_end,
    tok_a, tok_b, cot, cot_t, par_b, par_r, par_relay, weights,
    s1_out, s1_in, d_out, d_in, r_out, r_in, r_acc, own_acc, x_out, x_in,
    go_out, go_in, go_relay, pw_out, pw_in, nw_ref, act_acc, act_v,
    load_sem, tl_sem, ts_sem, tr_sem, cs_sem,
    wy_s, wy_r, wo_s, wo_r, wz_s, wz_r, wq_s, wq_r, wx_s, wx_r, wc_s, wc_r,
    s1_s, s1_r, d_s, d_r, r_s, r_r, x_s, x_r,
    gp_sem, gw_sem, go_s, go_r, gl_s, gl_r, gq_s, gq_r, sa_sem, nw_sem,
):
    r = lax.axis_index("replica")
    s = lax.axis_index("shard")
    c = lax.rem(s, 2)
    x = lax.rem(lax.div(s, 2), 2)
    y = lax.div(s, 4)
    ys = [lax.rem(y + 2, 4), lax.rem(y + 1, 4), lax.rem(y + 3, 4), y]

    def at(yy, xx, cc):
        return (r, (yy * 2 + xx) * 2 + cc)

    up, down = at(ys[1], x, c), at(ys[2], x, c)
    across, sibling = at(y, 1 - x, c), at(y, x, 1 - c)
    two_legs = offset == 1
    peer = s if not two_legs else at(y, 1 - x, c)[1]
    ahead = (lax.rem(r + offset, REPLICAS), peer)
    behind = (lax.rem(r + REPLICAS - offset, REPLICAS), peer)

    def remote(src, dst, ss, rs, to):
        return pltpu.make_async_remote_copy(
            src_ref=src, dst_ref=dst, send_sem=ss, recv_sem=rs, device_id=to, device_id_type=MESH
        )

    def columns(i, core):
        block = ys[i // 2] * 2 + (x if i % 2 == 0 else 1 - x)
        return pl.ds(pl.multiple_of((block * 2 + core) * ROWS, ROWS), ROWS)

    def place(i):
        return pl.ds(i * ROWS, ROWS)

    loads = [
        pltpu.make_async_copy(p_hbm, par, load_sem.at[0]),
        pltpu.make_async_copy(cot_hbm, cot.at[0], load_sem.at[1]),
        pltpu.make_async_copy(m_hbm, mom, load_sem.at[2]),
        pltpu.make_async_copy(v_hbm, sec, load_sem.at[3]),
    ]
    load_a = [
        pltpu.make_async_copy(
            tok_hbm.at[:, columns(i, c)], tok_a.at[pl.ds(0, TOK), place(i)], tl_sem.at[i // 2]
        )
        for i in range(8)
    ]
    load_b = [
        pltpu.make_async_copy(
            tok_hbm.at[:, columns(i, 1 - c)], tok_b.at[:, place(i)], tl_sem.at[4]
        )
        for i in range(8)
    ]
    loads[0].start()
    loads[1].start()
    for copy in load_a:
        copy.start()

    barrier = pltpu.get_barrier_semaphore()
    partners = [up, down, across, sibling, ahead, behind]
    back = (lax.rem(r + REPLICAS - 6, REPLICAS), s)
    if offset == 4:
        partners += [back, (lax.rem(r + 6, REPLICAS), s)]
    for to in partners:
        pl.semaphore_signal(barrier, inc=1, device_id=to, device_id_type=MESH)
    pl.semaphore_wait(barrier, len(partners))

    def quarter(q):
        return pl.ds(pl.multiple_of(q * QC, QC), QC)

    def swap_cot(q):
        return remote(
            cot_hbm.at[:, quarter(q)], cot.at[1, :, quarter(q)],
            ts_sem.at[1], cs_sem.at[q], sibling,
        )

    swap_tok = [
        remote(
            tok_hbm.at[:, columns(i, 1 - c)],
            tok_a.at[pl.ds(TOK, TOK), place(i)],
            ts_sem.at[0], tr_sem.at[i // 2], sibling,
        )
        for i in range(8)
    ]
    turns = sorted(range(QUARTERS), key=lambda q: order["issue_far"][q])
    swap_cot(turns[0]).start()
    for copy in swap_tok:
        copy.start()
    for q in turns[1:]:
        swap_cot(q).start()

    def w(q, i, parity=0):
        return weights.at[q, parity, place(i), :]

    def w_half(q, i, h):
        return weights.at[q, 0, pl.ds(i * ROWS + h * HALF, HALF), :]

    def send_w_y(q):
        return [
            remote(w(q, OWN), w(q, PRV), wy_s.at[0], wy_r.at[q], up),
            remote(w(q, OWN), w(q, NXT), wy_s.at[0], wy_r.at[q], down),
        ]

    def send_w_opp(q):
        return [
            remote(w_half(q, PRV, 0), w_half(q, OPP, 0), wo_s.at[0], wo_r.at[q], up),
            remote(w_half(q, NXT, 1), w_half(q, OPP, 1), wo_s.at[0], wo_r.at[q], down),
        ]

    def send_w_z(q):
        return [
            remote(w(q, OWN + 1), w(q, PRV + 1), wz_s.at[0], wz_r.at[q], up),
            remote(w(q, OWN + 1), w(q, NXT + 1), wz_s.at[0], wz_r.at[q], down),
        ]

    def send_w_far(q):
        return [
            remote(
                w_half(q, PRV + 1, 0), w_half(q, OPP + 1, 0), wq_s.at[0], wq_r.at[q], up
            ),
            remote(
                w_half(q, NXT + 1, 1), w_half(q, OPP + 1, 1), wq_s.at[0], wq_r.at[q], down
            ),
        ]

    def send_w_x(q, i):
        g = i // 2
        return remote(w(q, i), w(q, i + 1), wx_s.at[0], wx_r.at[q, g], across)

    def send_w_core(q, i):
        return remote(w(q, i), w(q, i, 1), wc_s.at[0], wc_r.at[q, min(i // 2, 1)], sibling)

    def send_s1(q):
        return [
            remote(s1_out.at[q, h], s1_in.at[q, h], s1_s.at[0], s1_r.at[q], to)
            for h, to in enumerate((up, down))
        ]

    def send_d(q):
        return [
            remote(d_out.at[q, h], d_in.at[q, h], d_s.at[0], d_r.at[q], to)
            for h, to in enumerate((up, down))
        ]

    def send_r(q):
        return [
            remote(r_out.at[q, h], r_in.at[q, h], r_s.at[0], r_r.at[q], to)
            for h, to in enumerate((up, down))
        ]

    def send_x(q):
        return remote(x_out.at[q], x_in.at[q], x_s.at[0], x_r.at[q], across)

    two_ways = offset == 4
    near_half, far_half = pl.ds(0, ROWS // 2), pl.ds(ROWS // 2, ROWS // 2)
    if two_ways:
        send_p = remote(
            par_b.at[near_half], par_r.at[near_half], gp_sem.at[0], gp_sem.at[1], ahead
        )
        leg_one = remote(par_b.at[far_half], par_relay, gp_sem.at[2], gp_sem.at[3], back)
        leg_two = remote(par_relay, par_r.at[far_half], gp_sem.at[4], gp_sem.at[5], back)
    else:
        send_p = remote(par_b, par_r, gp_sem.at[0], gp_sem.at[1], ahead)
    send_pw = remote(pw_out, pw_in, gw_sem.at[0], gw_sem.at[1], ahead)

    def send_go(q):
        source = go_relay if two_legs else go_out
        return remote(source.at[q], go_in.at[q], go_s.at[0], go_r.at[q], ahead)

    states = pl.ds(0, 2)

    def leg_states(q):
        return remote(
            go_out.at[q], go_relay.at[q, states], gl_s.at[0], gl_r.at[q], across
        )

    def leg_params(q):
        return remote(
            par_b.at[:, quarter(q)], go_relay.at[q, 2], gq_s.at[0], gq_r.at[q], across
        )

    loads[0].wait()
    par_b[...] = par[...].astype(BF16)
    if two_ways:
        leg_one.start()
    if not two_legs:
        send_p.start()
    pw_out[...] = jnp.full(pw_out.shape, pw_ref[0], F32)
    send_pw.start()

    @pl.loop(0, QUARTERS)
    def _(q):
        weights[q, 0, place(OWN), :] = (par[:, quarter(q)] / pw_ref[0]).astype(BF16)

    loads[2].start()
    loads[3].start()
    for copy in load_b:
        copy.start()

    def ended(ref, sem):
        pltpu.make_async_copy(ref, ref, sem).wait()

    def tokens_ready(group):
        pair = pl.ds(group * 2 * ROWS, 2 * ROWS)
        ended(tok_a.at[pl.ds(0, TOK), pair], tl_sem.at[group])
        ended(tok_a.at[pl.ds(TOK, TOK), pair], tr_sem.at[group])

    def product(q, group):
        return jnp.dot(
            cot_t[q], tok_a[:, pl.ds(group * 2 * ROWS, 2 * ROWS)], preferred_element_type=F32
        )

    def weights_y(q, first):
        for copy in send_w_y(q):
            copy.start()

    def weights_x(q, first):
        send_w_x(q, OWN).start()

    def issue_far(q, first):
        @pl.when(first)
        def _():
            loads[1].wait()
            tokens_ready(0)

        swap_cot(q).wait_recv()
        for n in range(2):
            cot_t[q, :, pl.ds(n * TOK, TOK)] = cot[n, :, quarter(q)].T
        far = product(q, 0)
        s1_out[q, 0] = far[:HALF].astype(BF16)
        s1_out[q, 1] = far[HALF:].astype(BF16)
        for copy in send_s1(q):
            copy.start()

    def issue_near(q, first):
        @pl.when(first)
        def _():
            tokens_ready(1)

        after = product(q, 1)
        d_out[q, 0] = after[HALF:].astype(BF16)
        send_d(q)[0].start()
        r_acc[q, 0] = after[:HALF]

        @pl.when(first)
        def _():
            tokens_ready(2)

        before = product(q, 2)
        d_out[q, 1] = before[:HALF].astype(BF16)
        send_d(q)[1].start()
        r_acc[q, 1] = before[HALF:]

    def issue_own(q, first):
        @pl.when(first)
        def _():
            tokens_ready(3)

        own_acc[q] = product(q, 3)

    def relay(q, first):
        ended(s1_in.at[q], s1_r.at[q])
        for n in range(2):
            r_out[q, n] = (r_acc[q, n] + s1_in[q, n].astype(F32)).astype(BF16)
            send_r(q)[n].start()

    def gather_sum(q, first):
        ended(d_in.at[q], d_r.at[q])
        ended(r_in.at[q], r_r.at[q])
        top = own_acc[q, :HALF] + r_in[q, 0].astype(F32) + d_in[q, 1].astype(F32)
        low = own_acc[q, HALF:] + d_in[q, 0].astype(F32) + r_in[q, 1].astype(F32)
        x_out[q, :HALF] = top[:, ROWS:].astype(BF16)
        x_out[q, HALF:] = low[:, ROWS:].astype(BF16)
        send_x(q).start()
        own_acc[q, :HALF, :ROWS] = top[:, :ROWS]
        own_acc[q, HALF:, :ROWS] = low[:, :ROWS]

    def update(q, first):
        @pl.when(first)
        def _():
            loads[2].wait()
            loads[3].wait()

        send_x(q).wait_recv()
        gradient = (own_acc[q, :, :ROWS] + x_in[q].astype(F32)).T
        fresh = beta_one * mom[:, quarter(q)] + (1.0 - beta_one) * gradient
        second = beta_two * sec[:, quarter(q)] + (1.0 - beta_two) * (gradient * gradient)
        go_out[q, 0] = fresh.astype(BF16)
        go_out[q, 1] = second.astype(BF16)
        (leg_states if two_legs else send_go)(q).start()
        mom[:, quarter(q)] = fresh
        sec[:, quarter(q)] = second
        par[:, quarter(q)] = adam(par[:, quarter(q)], fresh, second)

    def near_y(q, first):
        ended(weights.at[q, 0, pl.ds(NXT * ROWS, 2 * ROWS)], wy_r.at[q])
        onward = send_w_opp(q)
        for n, i in ((0, PRV), (1, NXT)):
            onward[n].start()
            send_w_core(q, i).start()

    def near_y_to_x(q, first):
        send_w_x(q, PRV).start()
        send_w_x(q, NXT).start()

    def across_own(q, first):
        send_w_x(q, OWN).wait_recv()
        send_w_core(q, OWN + 1).start()

    def across_to_y(q, first):
        for copy in send_w_z(q):
            copy.start()

    def far_y(q, first):
        ended(w(q, OPP), wo_r.at[q])
        send_w_x(q, OPP).start()
        send_w_core(q, OPP).start()

    def across_near(q, first):
        for i in (PRV, NXT):
            send_w_x(q, i).wait_recv()
            send_w_core(q, i + 1).start()

    def across_far(q, first):
        send_w_x(q, OPP).wait_recv()
        send_w_core(q, OPP + 1).start()

    def near_z(q, first):
        ended(weights.at[q, 0, pl.ds(NXT * ROWS, 2 * ROWS)], wz_r.at[q])
        onward = send_w_far(q)
        for n, i in ((0, PRV + 1), (1, NXT + 1)):
            onward[n].start()
            send_w_core(q, i).start()

    def far_both(q, first):
        ended(w(q, OPP), wo_r.at[q])
        send_w_core(q, OPP).start()
        ended(w(q, OPP + 1), wq_r.at[q])
        send_w_core(q, OPP + 1).start()

    def activation_part(q, slots, rows):
        total = jnp.dot(tok_a[rows, slots], weights[q, 0, slots], preferred_element_type=F32)
        return total + jnp.dot(
            tok_b[rows, slots], weights[q, 1, slots], preferred_element_type=F32
        )

    def halves(body):
        @pl.loop(0, 2)
        def _(n):
            body(pl.ds(pl.multiple_of(n * (TOK // 2), TOK // 2), TOK // 2))

    last, others = pl.ds(0, 2 * ROWS), pl.ds(2 * ROWS, 6 * ROWS)

    def activation_most(q, first):
        @pl.when(first)
        def _():
            ended(tok_b, tl_sem.at[4])

        ended(weights.at[q, 1, others], wc_r.at[q, 1])

        @halves
        def _(rows):
            act_acc[q, rows] = activation_part(q, others, rows)

    def activation_rest(q, first):
        ended(weights.at[q, 1, last], wc_r.at[q, 0])

        @halves
        def _(rows):
            total = act_acc[q, rows] + activation_part(q, last, rows)
            act_v[q, rows] = total.astype(BF16)

        @pl.when(q == QUARTERS - 1)
        def _():
            act_end[...] = act_v[q]

        @pl.when(q < QUARTERS - 1)
        def _():
            store_act(q).start()

    store_nw = pltpu.make_async_copy(nw_ref, nw_hbm, nw_sem.at[0])

    def store_act(q):
        return pltpu.make_async_copy(act_v.at[q], act_hbm.at[:, quarter(q)], sa_sem.at[q])

    def params_x(q, first):
        leg_params(q).start()

    def pass_on(q, first):
        leg_params(q).wait_recv()
        leg_states(q).wait_recv()
        send_go(q).start()

    def turn_back(q, first):
        leg_one.wait_recv()
        leg_two.start()

    def mix(q, first):
        @pl.when(first)
        def _():
            if not two_legs:
                send_p.wait_recv()
            if two_ways:
                leg_two.wait_recv()
            send_pw.wait_recv()
            nw_ref[0] = 0.5 * (pw_ref[0] + pw_in[0, 0])
            store_nw.start()

        send_go(q).wait_recv()
        theirs = go_in[q, 0].astype(F32)
        second = go_in[q, 1].astype(F32)
        param = go_in[q, 2] if two_legs else par_r[:, quarter(q)]
        stepped = adam(param.astype(F32), theirs, second)
        par[:, quarter(q)] = 0.5 * (par[:, quarter(q)] + stepped)
        mom[:, quarter(q)] = 0.5 * (mom[:, quarter(q)] + theirs)
        sec[:, quarter(q)] = 0.5 * (sec[:, quarter(q)] + second)

    events = {
        event.__name__: event
        for event in (
            weights_y, weights_x, issue_far, issue_near, issue_own, relay, gather_sum, update,
            near_y, near_y_to_x, across_own, across_to_y, far_y, across_near, across_far,
            near_z, far_both, activation_most, activation_rest, mix, turn_back,
            params_x, pass_on,
        )
    }
    for n in turns:
        send_w_core(n, OWN).start()

    def run(i, _):
        for name, places in order.items():
            places = {q: n for q, n in enumerate(places) if n >= 0}
            here = functools.reduce(jnp.logical_or, [i == n for n in places.values()])
            event = events[name]

            @pl.when(here)
            def _():
                turns_here = [turn * (i == n).astype(jnp.int32) for turn, n in places.items()]
                event(functools.reduce(jnp.add, turns_here), i == min(places.values()))

        return 0

    passes = 1 + max(max(places) for places in order.values())
    lax.fori_loop(0, passes, run, 0)

    def finish():
        around = sum(n >= 0 for n in order.get("across_to_y", ()))
        across = QUARTERS + 3 * (QUARTERS - around)
        ended(tok_a.at[pl.ds(TOK, TOK)], ts_sem.at[0])
        ended(cot.at[1], ts_sem.at[1])
        ended(weights.at[:, 0], wc_s.at[0])
        ended(weights.at[0, 0], wy_s.at[0])
        ended(weights.at[0, 0, pl.ds(0, 4 * ROWS)], wo_s.at[0])
        if around:
            ended(weights.at[0, 0, pl.ds(0, 2 * around * ROWS)], wz_s.at[0])
            ended(weights.at[0, 0, pl.ds(0, around * ROWS)], wq_s.at[0])
        ended(tok_b.at[pl.ds(0, across * (TOK // 16))], wx_s.at[0])
        ended(s1_out, s1_s.at[0])
        ended(d_out, d_s.at[0])
        ended(r_out, r_s.at[0])
        ended(x_out, x_s.at[0])
        if two_legs:
            ended(go_out, gl_s.at[0])
            ended(par_b, gq_s.at[0])
            ended(go_relay, go_s.at[0])
        else:
            ended(go_out, go_s.at[0])
            send_p.wait_send()
        send_pw.wait_send()
        for q in range(QUARTERS - 1):
            store_act(q).wait()
        store_nw.wait()
        if two_ways:
            leg_one.wait_send()
            leg_two.wait_send()

    finish()


def leave_kernel(*refs):
    states, act_end, act, new_states, new_act = refs[:3], refs[3], refs[4], refs[5:8], refs[8]
    held, sems = refs[9:]
    blocks = [pl.ds(n * TOK // 4, TOK // 4) for n in range(4)]
    early, late = pl.ds(0, FF - QC), pl.ds(FF - QC, QC)
    loads = [
        pltpu.make_async_copy(act.at[rows], held.at[rows], sems.at[n])
        for n, rows in enumerate(blocks)
    ]
    copies = [
        pltpu.make_async_copy(src, dst, sems.at[8 + n])
        for n, (src, dst) in enumerate(zip(states, new_states))
    ]
    copies.append(pltpu.make_async_copy(act_end, new_act.at[:, late], sems.at[11]))
    stores = [
        pltpu.make_async_copy(held.at[rows], new_act.at[rows, early], sems.at[4 + n])
        for n, rows in enumerate(blocks)
    ]
    for copy in loads + copies:
        copy.start()
    for load, store in zip(loads, stores):
        load.wait()
        store.start()
    for copy in copies + stores:
        copy.wait()


def leave(states, act, act_end):
    held = [pltpu.with_memory_space_constraint(a, pltpu.VMEM) for a in (*states, act_end)]
    shapes = [jax.ShapeDtypeStruct(a.shape, a.dtype) for a in states]
    return pl.pallas_call(
        leave_kernel,
        out_shape=(*shapes, jax.ShapeDtypeStruct((TOK, FF), BF16)),
        in_specs=[pl.BlockSpec(memory_space=pltpu.VMEM)] * len(held)
        + [pl.BlockSpec(memory_space=pl.ANY)],
        out_specs=tuple(pl.BlockSpec(memory_space=pl.ANY) for _ in range(4)),
        scratch_shapes=[pltpu.VMEM((TOK, FF - QC), BF16), pltpu.SemaphoreType.DMA((12,))],
        compiler_params=pltpu.CompilerParams(vmem_limit_bytes=8 << 20),
        name="leave",
    )(*held, act)


def step_kernel(offset, collective_id):
    any_spec = pl.BlockSpec(memory_space=pl.ANY)
    smem = pl.BlockSpec(memory_space=pltpu.SMEM)
    vmem = pl.BlockSpec(memory_space=pltpu.VMEM)
    Q = QUARTERS
    dma = pltpu.SemaphoreType.DMA
    scratch = [
        pltpu.VMEM((2 * TOK, 8 * ROWS), BF16),
        pltpu.VMEM((TOK, 8 * ROWS), BF16),
        pltpu.VMEM((2, TOK, FF), BF16),
        pltpu.VMEM((Q, QC, 2 * TOK), BF16),
        pltpu.VMEM((ROWS, FF), BF16),
        pltpu.VMEM((ROWS, FF), BF16),
        pltpu.VMEM((ROWS // 2, FF), BF16),
        pltpu.VMEM((Q, 2, 8 * ROWS, QC), BF16),
    ]
    scratch += [pltpu.VMEM((Q, 2, HALF, 2 * ROWS), BF16)] * 6
    scratch += [
        pltpu.VMEM((Q, 2, HALF, 2 * ROWS), F32),
        pltpu.VMEM((Q, QC, 2 * ROWS), F32),
        pltpu.VMEM((Q, QC, ROWS), BF16),
        pltpu.VMEM((Q, QC, ROWS), BF16),
        pltpu.VMEM((Q, 2, ROWS, QC), BF16),
        pltpu.VMEM((Q, 3 if offset == 1 else 2, ROWS, QC), BF16),
        pltpu.VMEM((Q, 3, ROWS, QC) if offset == 1 else (16, 128), BF16),
        pltpu.VMEM((8, 128), F32),
        pltpu.VMEM((8, 128), F32),
        pltpu.SMEM((1,), F32),
        pltpu.VMEM((Q, TOK, QC), F32),
        pltpu.VMEM((Q, TOK, QC), BF16),
        dma((4,)), dma((5,)), dma((2,)), dma((4,)), dma((Q,)),
        dma((1,)), dma((Q,)), dma((1,)), dma((Q,)),
        dma((1,)), dma((Q,)), dma((1,)), dma((Q,)),
        dma((1,)), dma((Q, 4)), dma((1,)), dma((Q, 2)),
        dma((1,)), dma((Q,)), dma((1,)), dma((Q,)), dma((1,)), dma((Q,)),
        dma((1,)), dma((Q,)),
        dma((6,)), dma((2,)), dma((1,)), dma((Q,)), dma((1,)), dma((Q,)), dma((1,)), dma((Q,)),
        dma((Q,)), dma((1,)),
    ]
    return pl.pallas_call(
        functools.partial(kernel, offset, ORDERS[offset]),
        out_shape=(
            pltpu.VMEM((ROWS, FF), F32),
            pltpu.VMEM((ROWS, FF), F32),
            pltpu.VMEM((ROWS, FF), F32),
            jax.ShapeDtypeStruct((1,), F32),
            jax.ShapeDtypeStruct((TOK, FF - QC), BF16),
            pltpu.VMEM((TOK, QC), BF16),
        ),
        in_specs=[any_spec, any_spec, any_spec, smem, any_spec, any_spec],
        out_specs=(vmem, vmem, vmem, any_spec, any_spec, vmem),
        scratch_shapes=scratch,
        compiler_params=pltpu.CompilerParams(
            collective_id=collective_id, has_side_effects=True, vmem_limit_bytes=48 << 20
        ),
        name=f"push_step_{offset}",
    )


def per_device(params, first_moment, second_moment, push_weight, tokens, cotangent, gossip_round):
    levels = REPLICAS.bit_length() - 1
    branches = [step_kernel(1 << level, level + 1) for level in range(levels)]
    new_params, new_first, new_second, new_weight, act, act_end = lax.switch(
        gossip_round[0] & (levels - 1),
        branches,
        params[0], first_moment[0], second_moment[0], push_weight, tokens[0], cotangent[0],
    )
    new_params, new_first, new_second, activation = leave(
        (new_params, new_first, new_second), act, act_end
    )
    return (new_params[None], new_first[None], new_second[None], new_weight, activation[None])


def solution(mesh):
    rows = P("replica", "shard", None)
    return jax.shard_map(
        per_device,
        mesh=mesh,
        in_specs=(rows, rows, rows, P("replica"), rows, rows, P()),
        out_specs=(rows, rows, rows, P("replica"), rows),
        check_vma=False,
    )
```

```python
import functools

import jax
import jax.numpy as jnp
from jax import lax
from jax.experimental import pallas as pl
from jax.experimental.pallas import tpu as pltpu
from jax.sharding import PartitionSpec as P

STEP_COUNT = 20

beta_one = 0.9
beta_two = 0.999
rate = 0.003
epsilon = 1e-08

MESH = pl.DeviceIdType.MESH
REPLICAS = 16
ROWS = 256
FF = 1024
TOK = 512
QUARTERS = 4
QC = FF // QUARTERS
HALF = QC // 2
F32 = jnp.float32
BF16 = jnp.bfloat16

OPP, NXT, PRV, OWN = 0, 2, 4, 6


ORDERS = {
    1: dict(
        across_far=(-1, -1, -1, 24),
        across_own=(12, 3, 7, 21),
        weights_y=(20, 13, 12, 2),
        gather_sum=(14, 8, 10, 15),
        issue_far=(7, 2, 4, 8),
        params_x=(6, 3, 9, 5),
        weights_x=(2, 1, 0, 20),
        near_y_to_x=(-1, -1, -1, 20),
        across_to_y=(16, 15, 13, -1),
        update=(16, 10, 11, 17),
        near_z=(21, 19, 20, -1),
        activation_most=(23, 20, 22, 24),
        across_near=(-1, -1, -1, 23),
        activation_rest=(24, 21, 23, 25),
        far_y=(-1, -1, -1, 20),
        pass_on=(18, 13, 14, 20),
        issue_near=(10, 2, 5, 11),
        relay=(10, 4, 6, 11),
        issue_own=(9, 3, 6, 8),
        mix=(21, 17, 18, 25),
        near_y=(21, 19, 20, 11),
        far_both=(23, 20, 22, -1),
    ),
    2: dict(
        activation_most=(11, 20, 13, 21),
        across_near=(10, 19, 9, -1),
        far_y=(5, 19, 10, -1),
        near_z=(-1, -1, -1, 20),
        relay=(10, 15, 4, 12),
        near_y=(3, 16, 4, 19),
        near_y_to_x=(3, 16, 4, -1),
        issue_far=(5, 13, 3, 7),
        across_far=(10, 20, 13, -1),
        gather_sum=(13, 17, 8, 14),
        weights_x=(1, 10, 2, 14),
        issue_near=(9, 14, 3, 10),
        activation_rest=(12, 20, 13, 21),
        issue_own=(8, 13, 3, 7),
        update=(13, 19, 11, 15),
        weights_y=(0, 13, 2, 16),
        mix=(18, 21, 13, 17),
        far_both=(-1, -1, -1, 20),
        across_own=(5, 15, 6, 18),
        across_to_y=(-1, -1, -1, 18),
    ),
    4: dict(
        issue_near=(5, 2, 10, 6),
        issue_own=(4, 2, 9, 6),
        weights_x=(3, 0, 2, 1),
        relay=(5, 2, 10, 7),
        far_both=(17, -1, -1, -1),
        weights_y=(11, 0, 9, 12),
        across_to_y=(14, -1, -1, -1),
        across_near=(-1, 7, 16, 17),
        far_y=(-1, 7, 15, 16),
        near_y=(14, 3, 10, 15),
        issue_far=(2, 1, 8, 5),
        near_y_to_x=(-1, 5, 10, 15),
        update=(7, 5, 14, 11),
        across_far=(-1, 9, 16, 19),
        activation_most=(16, 8, 17, 19),
        across_own=(6, 2, 10, 12),
        near_z=(15, -1, -1, -1),
        turn_back=(5, -1, -1, -1),
        gather_sum=(6, 3, 13, 9),
        activation_rest=(18, 9, 17, 19),
        mix=(13, 12, 19, 15),
    ),
    8: dict(
        across_own=(12, 4, 9, 15),
        weights_y=(11, 0, 1, 15),
        across_to_y=(-1, -1, -1, 15),
        far_y=(16, 4, 11, -1),
        activation_rest=(18, 6, 15, 19),
        issue_own=(11, 5, 4, 9),
        weights_x=(1, 3, 2, 7),
        update=(17, 10, 6, 13),
        issue_far=(9, 4, 3, 6),
        gather_sum=(15, 7, 4, 10),
        across_far=(17, 5, 14, -1),
        near_z=(-1, -1, -1, 17),
        near_y=(14, 2, 8, 17),
        activation_most=(16, 5, 13, 18),
        across_near=(15, 4, 12, -1),
        near_y_to_x=(14, 3, 8, -1),
        issue_near=(12, 4, 3, 7),
        relay=(13, 5, 3, 7),
        far_both=(-1, -1, -1, 18),
        mix=(19, 15, 12, 18),
    ),
}


def adam(param, first, second):
    correct_one = 1.0 - beta_one ** (STEP_COUNT + 1)
    correct_two = 1.0 - beta_two ** (STEP_COUNT + 1)
    scaled = first * (rate / correct_one)
    return param - scaled / (jnp.sqrt(second * (1.0 / correct_two)) + epsilon)


def kernel(
    offset, order,
    p_hbm, m_hbm, v_hbm, pw_hbm, tok_hbm, cot_hbm,
    par, mom, sec, nw_hbm, act_hbm, act_end,
    tok_a, tok_b, cot, cot_t, par_b, par_r, par_relay, weights,
    s1_out, s1_in, d_out, d_in, r_out, r_in, r_acc, own_acc, x_out, x_in,
    go_out, go_in, go_relay, pw_out, pw_in, pw_ref, nw_ref, act_acc, act_v,
    load_sem, tl_sem, ts_sem, tr_sem, cs_sem,
    wy_s, wy_r, wo_s, wo_r, wz_s, wz_r, wq_s, wq_r, wx_s, wx_r, wc_s, wc_r,
    s1_s, s1_r, d_s, d_r, r_s, r_r, x_s, x_r,
    gp_sem, gw_sem, go_s, go_r, gl_s, gl_r, gq_s, gq_r, sa_sem, nw_sem,
):
    r = lax.axis_index("replica")
    s = lax.axis_index("shard")
    c = lax.rem(s, 2)
    x = lax.rem(lax.div(s, 2), 2)
    y = lax.div(s, 4)
    ys = [lax.rem(y + 2, 4), lax.rem(y + 1, 4), lax.rem(y + 3, 4), y]

    def at(yy, xx, cc):
        return (r, (yy * 2 + xx) * 2 + cc)

    up, down = at(ys[1], x, c), at(ys[2], x, c)
    across, sibling = at(y, 1 - x, c), at(y, x, 1 - c)
    two_legs = offset == 1
    peer = s if not two_legs else at(y, 1 - x, c)[1]
    ahead = (lax.rem(r + offset, REPLICAS), peer)
    behind = (lax.rem(r + REPLICAS - offset, REPLICAS), peer)

    def remote(src, dst, ss, rs, to):
        return pltpu.make_async_remote_copy(
            src_ref=src, dst_ref=dst, send_sem=ss, recv_sem=rs, device_id=to, device_id_type=MESH
        )

    def columns(i, core):
        block = ys[i // 2] * 2 + (x if i % 2 == 0 else 1 - x)
        return pl.ds(pl.multiple_of((block * 2 + core) * ROWS, ROWS), ROWS)

    def place(i):
        return pl.ds(i * ROWS, ROWS)

    loads = [
        pltpu.make_async_copy(p_hbm, par, load_sem.at[0]),
        pltpu.make_async_copy(cot_hbm, cot.at[0], load_sem.at[1]),
        pltpu.make_async_copy(m_hbm, mom, load_sem.at[2]),
        pltpu.make_async_copy(v_hbm, sec, load_sem.at[3]),
        pltpu.make_async_copy(pw_hbm, pw_ref, load_sem.at[4]),
    ]
    load_a = [
        pltpu.make_async_copy(
            tok_hbm.at[:, columns(i, c)], tok_a.at[pl.ds(0, TOK), place(i)], tl_sem.at[i // 2]
        )
        for i in range(8)
    ]
    load_b = [
        pltpu.make_async_copy(
            tok_hbm.at[:, columns(i, 1 - c)], tok_b.at[:, place(i)], tl_sem.at[4]
        )
        for i in range(8)
    ]
    barrier = pltpu.get_barrier_semaphore()
    partners = [up, down, across, sibling, ahead, behind]
    back = (lax.rem(r + REPLICAS - 6, REPLICAS), s)
    if offset == 4:
        partners += [back, (lax.rem(r + 6, REPLICAS), s)]
    for to in partners:
        pl.semaphore_signal(barrier, inc=1, device_id=to, device_id_type=MESH)
    loads[0].start()
    loads[4].start()
    loads[1].start()
    for copy in load_a:
        copy.start()
    pl.semaphore_wait(barrier, len(partners))

    def quarter(q):
        return pl.ds(pl.multiple_of(q * QC, QC), QC)

    def swap_cot(q):
        return remote(
            cot_hbm.at[:, quarter(q)], cot.at[1, :, quarter(q)],
            ts_sem.at[1], cs_sem.at[q], sibling,
        )

    swap_tok = [
        remote(
            tok_hbm.at[:, columns(i, 1 - c)],
            tok_a.at[pl.ds(TOK, TOK), place(i)],
            ts_sem.at[0], tr_sem.at[i // 2], sibling,
        )
        for i in range(8)
    ]
    turns = sorted(range(QUARTERS), key=lambda q: order["issue_far"][q])
    swap_cot(turns[0]).start()
    for copy in swap_tok:
        copy.start()
    for q in turns[1:]:
        swap_cot(q).start()

    def w(q, i, parity=0):
        return weights.at[q, parity, place(i), :]

    def w_half(q, i, h):
        return weights.at[q, 0, pl.ds(i * ROWS + h * HALF, HALF), :]

    def send_w_y(q):
        return [
            remote(w(q, OWN), w(q, PRV), wy_s.at[0], wy_r.at[q], up),
            remote(w(q, OWN), w(q, NXT), wy_s.at[0], wy_r.at[q], down),
        ]

    def send_w_opp(q):
        return [
            remote(w_half(q, PRV, 0), w_half(q, OPP, 0), wo_s.at[0], wo_r.at[q], up),
            remote(w_half(q, NXT, 1), w_half(q, OPP, 1), wo_s.at[0], wo_r.at[q], down),
        ]

    def send_w_z(q):
        return [
            remote(w(q, OWN + 1), w(q, PRV + 1), wz_s.at[0], wz_r.at[q], up),
            remote(w(q, OWN + 1), w(q, NXT + 1), wz_s.at[0], wz_r.at[q], down),
        ]

    def send_w_far(q):
        return [
            remote(
                w_half(q, PRV + 1, 0), w_half(q, OPP + 1, 0), wq_s.at[0], wq_r.at[q], up
            ),
            remote(
                w_half(q, NXT + 1, 1), w_half(q, OPP + 1, 1), wq_s.at[0], wq_r.at[q], down
            ),
        ]

    def send_w_x(q, i):
        g = i // 2
        return remote(w(q, i), w(q, i + 1), wx_s.at[0], wx_r.at[q, g], across)

    def send_w_core(q, i):
        return remote(w(q, i), w(q, i, 1), wc_s.at[0], wc_r.at[q, min(i // 2, 1)], sibling)

    def send_s1(q):
        return [
            remote(s1_out.at[q, h], s1_in.at[q, h], s1_s.at[0], s1_r.at[q], to)
            for h, to in enumerate((up, down))
        ]

    def send_d(q):
        return [
            remote(d_out.at[q, h], d_in.at[q, h], d_s.at[0], d_r.at[q], to)
            for h, to in enumerate((up, down))
        ]

    def send_r(q):
        return [
            remote(r_out.at[q, h], r_in.at[q, h], r_s.at[0], r_r.at[q], to)
            for h, to in enumerate((up, down))
        ]

    def send_x(q):
        return remote(x_out.at[q], x_in.at[q], x_s.at[0], x_r.at[q], across)

    two_ways = offset == 4
    near_half, far_half = pl.ds(0, ROWS // 2), pl.ds(ROWS // 2, ROWS // 2)
    if two_ways:
        send_p = remote(
            par_b.at[near_half], par_r.at[near_half], gp_sem.at[0], gp_sem.at[1], ahead
        )
        leg_one = remote(par_b.at[far_half], par_relay, gp_sem.at[2], gp_sem.at[3], back)
        leg_two = remote(par_relay, par_r.at[far_half], gp_sem.at[4], gp_sem.at[5], back)
    else:
        send_p = remote(par_b, par_r, gp_sem.at[0], gp_sem.at[1], ahead)
    send_pw = remote(pw_out, pw_in, gw_sem.at[0], gw_sem.at[1], ahead)

    def send_go(q):
        source = go_relay if two_legs else go_out
        return remote(source.at[q], go_in.at[q], go_s.at[0], go_r.at[q], ahead)

    states = pl.ds(0, 2)

    def leg_states(q):
        return remote(
            go_out.at[q], go_relay.at[q, states], gl_s.at[0], gl_r.at[q], across
        )

    def leg_params(q):
        return remote(
            par_b.at[:, quarter(q)], go_relay.at[q, 2], gq_s.at[0], gq_r.at[q], across
        )

    loads[0].wait()
    loads[4].wait()
    par_b[...] = par[...].astype(BF16)
    if two_ways:
        leg_one.start()
    if not two_legs:
        send_p.start()
    pw_out[...] = jnp.full(pw_out.shape, pw_ref[0], F32)
    send_pw.start()

    @pl.loop(0, QUARTERS)
    def _(q):
        weights[q, 0, place(OWN), :] = (par[:, quarter(q)] / pw_ref[0]).astype(BF16)

    loads[2].start()
    loads[3].start()
    for copy in load_b:
        copy.start()

    def ended(ref, sem):
        pltpu.make_async_copy(ref, ref, sem).wait()

    def tokens_ready(group):
        pair = pl.ds(group * 2 * ROWS, 2 * ROWS)
        ended(tok_a.at[pl.ds(0, TOK), pair], tl_sem.at[group])
        ended(tok_a.at[pl.ds(TOK, TOK), pair], tr_sem.at[group])

    def product(q, group):
        return jnp.dot(
            cot_t[q], tok_a[:, pl.ds(group * 2 * ROWS, 2 * ROWS)], preferred_element_type=F32
        )

    def weights_y(q, first):
        for copy in send_w_y(q):
            copy.start()

    def weights_x(q, first):
        send_w_x(q, OWN).start()

    def issue_far(q, first):
        @pl.when(first)
        def _():
            loads[1].wait()
            tokens_ready(0)

        swap_cot(q).wait_recv()
        for n in range(2):
            cot_t[q, :, pl.ds(n * TOK, TOK)] = cot[n, :, quarter(q)].T
        far = product(q, 0)
        s1_out[q, 0] = far[:HALF].astype(BF16)
        s1_out[q, 1] = far[HALF:].astype(BF16)
        for copy in send_s1(q):
            copy.start()

    def issue_near(q, first):
        @pl.when(first)
        def _():
            tokens_ready(1)

        after = product(q, 1)
        d_out[q, 0] = after[HALF:].astype(BF16)
        send_d(q)[0].start()
        r_acc[q, 0] = after[:HALF]

        @pl.when(first)
        def _():
            tokens_ready(2)

        before = product(q, 2)
        d_out[q, 1] = before[:HALF].astype(BF16)
        send_d(q)[1].start()
        r_acc[q, 1] = before[HALF:]

    def issue_own(q, first):
        @pl.when(first)
        def _():
            tokens_ready(3)

        own_acc[q] = product(q, 3)

    def relay(q, first):
        ended(s1_in.at[q], s1_r.at[q])
        for n in range(2):
            r_out[q, n] = (r_acc[q, n] + s1_in[q, n].astype(F32)).astype(BF16)
            send_r(q)[n].start()

    def gather_sum(q, first):
        ended(d_in.at[q], d_r.at[q])
        ended(r_in.at[q], r_r.at[q])
        top = own_acc[q, :HALF] + r_in[q, 0].astype(F32) + d_in[q, 1].astype(F32)
        low = own_acc[q, HALF:] + d_in[q, 0].astype(F32) + r_in[q, 1].astype(F32)
        x_out[q, :HALF] = top[:, ROWS:].astype(BF16)
        x_out[q, HALF:] = low[:, ROWS:].astype(BF16)
        send_x(q).start()
        own_acc[q, :HALF, :ROWS] = top[:, :ROWS]
        own_acc[q, HALF:, :ROWS] = low[:, :ROWS]

    def update(q, first):
        @pl.when(first)
        def _():
            loads[2].wait()
            loads[3].wait()

        send_x(q).wait_recv()
        gradient = (own_acc[q, :, :ROWS] + x_in[q].astype(F32)).T
        fresh = beta_one * mom[:, quarter(q)] + (1.0 - beta_one) * gradient
        second = beta_two * sec[:, quarter(q)] + (1.0 - beta_two) * (gradient * gradient)
        go_out[q, 0] = fresh.astype(BF16)
        go_out[q, 1] = second.astype(BF16)
        (leg_states if two_legs else send_go)(q).start()
        mom[:, quarter(q)] = fresh
        sec[:, quarter(q)] = second
        par[:, quarter(q)] = adam(par[:, quarter(q)], fresh, second)

    def near_y(q, first):
        ended(weights.at[q, 0, pl.ds(NXT * ROWS, 2 * ROWS)], wy_r.at[q])
        onward = send_w_opp(q)
        for n, i in ((0, PRV), (1, NXT)):
            onward[n].start()
            send_w_core(q, i).start()

    def near_y_to_x(q, first):
        send_w_x(q, PRV).start()
        send_w_x(q, NXT).start()

    def across_own(q, first):
        send_w_x(q, OWN).wait_recv()
        send_w_core(q, OWN + 1).start()

    def across_to_y(q, first):
        for copy in send_w_z(q):
            copy.start()

    def far_y(q, first):
        ended(w(q, OPP), wo_r.at[q])
        send_w_x(q, OPP).start()
        send_w_core(q, OPP).start()

    def across_near(q, first):
        for i in (PRV, NXT):
            send_w_x(q, i).wait_recv()
            send_w_core(q, i + 1).start()

    def across_far(q, first):
        send_w_x(q, OPP).wait_recv()
        send_w_core(q, OPP + 1).start()

    def near_z(q, first):
        ended(weights.at[q, 0, pl.ds(NXT * ROWS, 2 * ROWS)], wz_r.at[q])
        onward = send_w_far(q)
        for n, i in ((0, PRV + 1), (1, NXT + 1)):
            onward[n].start()
            send_w_core(q, i).start()

    def far_both(q, first):
        ended(w(q, OPP), wo_r.at[q])
        send_w_core(q, OPP).start()
        ended(w(q, OPP + 1), wq_r.at[q])
        send_w_core(q, OPP + 1).start()

    def activation_part(q, slots, rows):
        total = jnp.dot(tok_a[rows, slots], weights[q, 0, slots], preferred_element_type=F32)
        return total + jnp.dot(
            tok_b[rows, slots], weights[q, 1, slots], preferred_element_type=F32
        )

    def halves(body):
        @pl.loop(0, 2)
        def _(n):
            body(pl.ds(pl.multiple_of(n * (TOK // 2), TOK // 2), TOK // 2))

    last, others = pl.ds(0, 2 * ROWS), pl.ds(2 * ROWS, 6 * ROWS)

    def activation_most(q, first):
        @pl.when(first)
        def _():
            ended(tok_b, tl_sem.at[4])

        ended(weights.at[q, 1, others], wc_r.at[q, 1])

        @halves
        def _(rows):
            act_acc[q, rows] = activation_part(q, others, rows)

    def activation_rest(q, first):
        ended(weights.at[q, 1, last], wc_r.at[q, 0])

        @halves
        def _(rows):
            total = act_acc[q, rows] + activation_part(q, last, rows)
            act_v[q, rows] = total.astype(BF16)

        @pl.when(q == QUARTERS - 1)
        def _():
            act_end[...] = act_v[q]

        @pl.when(q < QUARTERS - 1)
        def _():
            store_act(q).start()

    store_nw = pltpu.make_async_copy(nw_ref, nw_hbm, nw_sem.at[0])

    def store_act(q):
        return pltpu.make_async_copy(act_v.at[q], act_hbm.at[:, quarter(q)], sa_sem.at[q])

    def params_x(q, first):
        leg_params(q).start()

    def pass_on(q, first):
        leg_params(q).wait_recv()
        leg_states(q).wait_recv()
        send_go(q).start()

    def turn_back(q, first):
        leg_one.wait_recv()
        leg_two.start()

    def mix(q, first):
        @pl.when(first)
        def _():
            if not two_legs:
                send_p.wait_recv()
            if two_ways:
                leg_two.wait_recv()
            send_pw.wait_recv()
            nw_ref[0] = 0.5 * (pw_ref[0] + pw_in[0, 0])
            store_nw.start()

        send_go(q).wait_recv()
        theirs = go_in[q, 0].astype(F32)
        second = go_in[q, 1].astype(F32)
        param = go_in[q, 2] if two_legs else par_r[:, quarter(q)]
        stepped = adam(param.astype(F32), theirs, second)
        par[:, quarter(q)] = 0.5 * (par[:, quarter(q)] + stepped)
        mom[:, quarter(q)] = 0.5 * (mom[:, quarter(q)] + theirs)
        sec[:, quarter(q)] = 0.5 * (sec[:, quarter(q)] + second)

    events = {
        event.__name__: event
        for event in (
            weights_y, weights_x, issue_far, issue_near, issue_own, relay, gather_sum, update,
            near_y, near_y_to_x, across_own, across_to_y, far_y, across_near, across_far,
            near_z, far_both, activation_most, activation_rest, mix, turn_back,
            params_x, pass_on,
        )
    }
    for n in turns:
        send_w_core(n, OWN).start()

    def run(i, _):
        for name, places in order.items():
            places = {q: n for q, n in enumerate(places) if n >= 0}
            here = functools.reduce(jnp.logical_or, [i == n for n in places.values()])
            event = events[name]

            @pl.when(here)
            def _():
                turns_here = [turn * (i == n).astype(jnp.int32) for turn, n in places.items()]
                event(functools.reduce(jnp.add, turns_here), i == min(places.values()))

        return 0

    passes = 1 + max(max(places) for places in order.values())
    lax.fori_loop(0, passes, run, 0)

    def finish():
        around = sum(n >= 0 for n in order.get("across_to_y", ()))
        across = QUARTERS + 3 * (QUARTERS - around)
        ended(tok_a.at[pl.ds(TOK, TOK)], ts_sem.at[0])
        ended(cot.at[1], ts_sem.at[1])
        ended(weights.at[:, 0], wc_s.at[0])
        ended(weights.at[0, 0], wy_s.at[0])
        ended(weights.at[0, 0, pl.ds(0, 4 * ROWS)], wo_s.at[0])
        if around:
            ended(weights.at[0, 0, pl.ds(0, 2 * around * ROWS)], wz_s.at[0])
            ended(weights.at[0, 0, pl.ds(0, around * ROWS)], wq_s.at[0])
        ended(tok_b.at[pl.ds(0, across * (TOK // 16))], wx_s.at[0])
        ended(s1_out, s1_s.at[0])
        ended(d_out, d_s.at[0])
        ended(r_out, r_s.at[0])
        ended(x_out, x_s.at[0])
        if two_legs:
            ended(go_out, gl_s.at[0])
            ended(par_b, gq_s.at[0])
            ended(go_relay, go_s.at[0])
        else:
            ended(go_out, go_s.at[0])
            send_p.wait_send()
        send_pw.wait_send()
        for q in range(QUARTERS - 1):
            store_act(q).wait()
        store_nw.wait()
        if two_ways:
            leg_one.wait_send()
            leg_two.wait_send()

    finish()


def leave_kernel(*refs):
    states, act_end, act, new_states, new_act = refs[:3], refs[3], refs[4], refs[5:8], refs[8]
    held, sems = refs[9:]
    blocks = [pl.ds(n * TOK // 4, TOK // 4) for n in range(4)]
    early, late = pl.ds(0, FF - QC), pl.ds(FF - QC, QC)
    loads = [
        pltpu.make_async_copy(act.at[rows], held.at[rows], sems.at[n])
        for n, rows in enumerate(blocks)
    ]
    copies = [
        pltpu.make_async_copy(src, dst, sems.at[8 + n])
        for n, (src, dst) in enumerate(zip(states, new_states))
    ]
    copies.append(pltpu.make_async_copy(act_end, new_act.at[:, late], sems.at[11]))
    stores = [
        pltpu.make_async_copy(held.at[rows], new_act.at[rows, early], sems.at[4 + n])
        for n, rows in enumerate(blocks)
    ]
    for copy in loads + copies:
        copy.start()
    for load, store in zip(loads, stores):
        load.wait()
        store.start()
    for copy in copies + stores:
        copy.wait()


def leave(states, act, act_end):
    held = [pltpu.with_memory_space_constraint(a, pltpu.VMEM) for a in (*states, act_end)]
    shapes = [jax.ShapeDtypeStruct(a.shape, a.dtype) for a in states]
    return pl.pallas_call(
        leave_kernel,
        out_shape=(*shapes, jax.ShapeDtypeStruct((TOK, FF), BF16)),
        in_specs=[pl.BlockSpec(memory_space=pltpu.VMEM)] * len(held)
        + [pl.BlockSpec(memory_space=pl.ANY)],
        out_specs=tuple(pl.BlockSpec(memory_space=pl.ANY) for _ in range(4)),
        scratch_shapes=[pltpu.VMEM((TOK, FF - QC), BF16), pltpu.SemaphoreType.DMA((12,))],
        compiler_params=pltpu.CompilerParams(vmem_limit_bytes=8 << 20),
        name="leave",
    )(*held, act)


def step_kernel(offset, collective_id):
    any_spec = pl.BlockSpec(memory_space=pl.ANY)
    vmem = pl.BlockSpec(memory_space=pltpu.VMEM)
    Q = QUARTERS
    dma = pltpu.SemaphoreType.DMA
    scratch = [
        pltpu.VMEM((2 * TOK, 8 * ROWS), BF16),
        pltpu.VMEM((TOK, 8 * ROWS), BF16),
        pltpu.VMEM((2, TOK, FF), BF16),
        pltpu.VMEM((Q, QC, 2 * TOK), BF16),
        pltpu.VMEM((ROWS, FF), BF16),
        pltpu.VMEM((ROWS, FF), BF16),
        pltpu.VMEM((ROWS // 2, FF), BF16),
        pltpu.VMEM((Q, 2, 8 * ROWS, QC), BF16),
    ]
    scratch += [pltpu.VMEM((Q, 2, HALF, 2 * ROWS), BF16)] * 6
    scratch += [
        pltpu.VMEM((Q, 2, HALF, 2 * ROWS), F32),
        pltpu.VMEM((Q, QC, 2 * ROWS), F32),
        pltpu.VMEM((Q, QC, ROWS), BF16),
        pltpu.VMEM((Q, QC, ROWS), BF16),
        pltpu.VMEM((Q, 2, ROWS, QC), BF16),
        pltpu.VMEM((Q, 3 if offset == 1 else 2, ROWS, QC), BF16),
        pltpu.VMEM((Q, 3, ROWS, QC) if offset == 1 else (16, 128), BF16),
        pltpu.VMEM((8, 128), F32),
        pltpu.VMEM((8, 128), F32),
        pltpu.SMEM((1,), F32),
        pltpu.SMEM((1,), F32),
        pltpu.VMEM((Q, TOK, QC), F32),
        pltpu.VMEM((Q, TOK, QC), BF16),
        dma((5,)), dma((5,)), dma((2,)), dma((4,)), dma((Q,)),
        dma((1,)), dma((Q,)), dma((1,)), dma((Q,)),
        dma((1,)), dma((Q,)), dma((1,)), dma((Q,)),
        dma((1,)), dma((Q, 4)), dma((1,)), dma((Q, 2)),
        dma((1,)), dma((Q,)), dma((1,)), dma((Q,)), dma((1,)), dma((Q,)),
        dma((1,)), dma((Q,)),
        dma((6,)), dma((2,)), dma((1,)), dma((Q,)), dma((1,)), dma((Q,)), dma((1,)), dma((Q,)),
        dma((Q,)), dma((1,)),
    ]
    return pl.pallas_call(
        functools.partial(kernel, offset, ORDERS[offset]),
        out_shape=(
            pltpu.VMEM((ROWS, FF), F32),
            pltpu.VMEM((ROWS, FF), F32),
            pltpu.VMEM((ROWS, FF), F32),
            jax.ShapeDtypeStruct((1,), F32),
            jax.ShapeDtypeStruct((TOK, FF - QC), BF16),
            pltpu.VMEM((TOK, QC), BF16),
        ),
        in_specs=[any_spec] * 6,
        out_specs=(vmem, vmem, vmem, any_spec, any_spec, vmem),
        scratch_shapes=scratch,
        compiler_params=pltpu.CompilerParams(
            collective_id=collective_id, has_side_effects=True, vmem_limit_bytes=48 << 20
        ),
        name=f"push_step_{offset}",
    )


def per_device(params, first_moment, second_moment, push_weight, tokens, cotangent, gossip_round):
    levels = REPLICAS.bit_length() - 1
    branches = [step_kernel(1 << level, level + 1) for level in range(levels)]
    new_params, new_first, new_second, new_weight, act, act_end = lax.switch(
        gossip_round[0] & (levels - 1),
        branches,
        params[0], first_moment[0], second_moment[0], push_weight, tokens[0], cotangent[0],
    )
    new_params, new_first, new_second, activation = leave(
        (new_params, new_first, new_second), act, act_end
    )
    return (new_params[None], new_first[None], new_second[None], new_weight, activation[None])


def solution(mesh):
    rows = P("replica", "shard", None)
    return jax.shard_map(
        per_device,
        mesh=mesh,
        in_specs=(rows, rows, rows, P("replica"), rows, rows, P()),
        out_specs=(rows, rows, rows, P("replica"), rows),
        check_vma=False,
    )
```
